256 devices in a mesh: genome: 16 (over x_hi, y, core), people: 16 (over z, x_lo).
Axes of the slice: x: 4 (x_hi: 2, x_lo: 2; x = x_hi * 2 + x_lo), y: 4, z: 8, core: 2. Of those that a mesh axis runs over, the one named last changes fastest.
Arguments:
- genotypes: bfloat16 [49152, 16384], P('people', 'genome'), may hold values from -6 to 6
- expression: bfloat16 [49152, 4096], P('people', 'genome'), may hold values from -6 to 6
- coef_start: float32 [4096, 2048], P('genome'), may hold values from -4 to 4
- penalty: float32 [4096], P('genome'), may hold values from 0.02 to 0.3
- step_size: float32 [4096], P('genome'), may hold values from 0.3 to 0.8
- window_start: int32 [4096], P('genome'), may hold values from 0 to 15872, as said below
- window_end: int32 [4096], P('genome'), may hold values from 512 to 16384, as said below
- active_blocks: int32 [4096, 16], P('genome'), may hold values 0 or 1
Outputs:
- coef: float32 [4096, 2048], P('genome')
- peaks: float32 [4096, 16], P('genome')
The draws below stay inside these ranges and needn't reach their ends.
Inputs may be any that keep to these rules, and one draw needn't show every extreme that they name: `window_start`: gene g's window lies within variants g // 256 * 1024 - 512 to (g // 256 + 1) * 1024 + 512 clipped to the region, and is not empty. window_end exceeds window_start by 512 or more.
All inputs are finite; a program needn't handle non-finite values. No bound on the sum of `active_blocks` on one device may be relied on, other than what follows from the above.
Results may differ from the reference program's by a relative error of at most 0.0035.
Values may be sent and summed in bfloat16 or wider, within the bound.
No kernel may reach another device: no remote copies, remote signals or barrier semaphores. Data moves between devices by JAX's collectives and lax.ppermute only.
A program may use at most 128 MiB of HBM per device.

```python
import math
import jax
import jax.numpy as jnp
from jax import lax

V_DEV = 1024
G_DEV = 256
HALO = 512
WIDTH = 2048
WB = 16
PEOPLE = 49152
VARIANTS = 16384
GENES = 4096
N_GENOME = 16


def window_pair(key):
    key = jax.random.fold_in(key, 11)
    first_key, second_key = jax.random.split(key)
    gene = jnp.arange(GENES, dtype=jnp.int32)
    base = gene // G_DEV * V_DEV - HALO
    offset = jax.random.randint(first_key, (GENES,), 0, V_DEV + 1)
    offset = jnp.where(gene == 0, 0, offset)
    offset = jnp.where(gene == GENES - 1, V_DEV, offset)
    extra = jax.random.randint(second_key, (GENES,), 0, WIDTH - V_DEV - offset + 1)
    extra = jnp.where(gene == 0, 0, extra)
    ending = offset + V_DEV + extra
    ending = jnp.where(gene == GENES - 1, WIDTH, ending)
    lower = jnp.clip(base + offset, 0, VARIANTS).astype(jnp.int32)
    upper = jnp.clip(base + ending, 0, VARIANTS).astype(jnp.int32)
    return (lower, upper)


def draw_window_start(key, part):
    lower, upper = window_pair(key)
    return lower


def draw_window_end(key, part):
    lower, upper = window_pair(key)
    return upper


def set_ends(result, stream_key, low, top_value):
    dims = result.shape
    spot = [jax.random.randint(jax.random.fold_in(stream_key, axis), (), 0, dims[axis]) for axis in range(len(dims))]
    result = result.at[tuple(spot)].set(low)
    longest = dims.index(max(dims))
    spot[longest] = (spot[longest] + 1) % dims[longest]
    return result.at[tuple(spot)].set(top_value)


def steps_of(stream_key, extent, cuts, smallest, top_value):
    loudness, own = 1.0, jax.random.fold_in(stream_key, 6)
    for position, parts in cuts:
        steps = jnp.exp(jax.random.uniform(jax.random.fold_in(own, position), (parts,), jnp.float32, smallest / len(cuts), top_value / len(cuts)))
        loudness = loudness * jnp.repeat(steps, extent[position] // parts).reshape([-1 if axis == position else 1 for axis in range(len(extent))])
    return loudness


def centred(rng, shape, width, bound, cuts=(), held_as=jnp.bfloat16):
    values = jax.random.normal(rng, shape, jnp.float32) * width
    if len(cuts) > 0:
        values = steps_of(rng, shape, cuts, -0.22, 0.18) * values
    return jnp.clip(values, min=-bound, max=bound).astype(held_as)


def setup_inputs(seed: int = 0) -> dict:
    streams_of = jax.random.split(jax.random.key(seed), 9)
    return {
        "genotypes": centred(streams_of[0], (PEOPLE, VARIANTS), 1.0, 6.0, ((0, 16), (1, 16))),
        "expression": centred(streams_of[1], (PEOPLE, GENES), 1.0, 6.0, ((0, 16), (1, 16))),
        "coef_start": centred(streams_of[2], (GENES, WIDTH), 0.5, 4.0, ((0, 16),), jnp.float32),
        "penalty": jnp.clip(jnp.exp(math.log(0.3) - 2.7080503 * jax.random.uniform(streams_of[3], (GENES,), jnp.float32) ** steps_of(streams_of[3], (GENES,), ((0, 16),), -0.2, 0.2)), 0.02, 0.3),
        "step_size": jnp.clip(0.3 + 0.5 * jax.random.uniform(streams_of[4], (GENES,), jnp.float32) ** steps_of(streams_of[4], (GENES,), ((0, 16),), -0.2, 0.2), 0.3, 0.8),
        "window_start": draw_window_start(jax.random.fold_in(streams_of[8], 71), 0),
        "window_end": draw_window_end(jax.random.fold_in(streams_of[8], 71), 0),
        "active_blocks": set_ends((jax.random.randint(streams_of[7], (GENES, WB), 0, 4) < 3).astype(jnp.int32), jax.random.fold_in(streams_of[7], 1), 0, 1),
    }


l1_share = 0.5


def shrink(coef, grad, penalty, step, mask):
    moved = coef + step[:, None] * grad
    cut = step[:, None] * penalty[:, None]
    kept = jnp.sign(moved) * jnp.maximum(jnp.abs(moved) - cut * l1_share, 0.0)
    return mask * kept / (1.0 + cut * (1.0 - l1_share))


def block_peaks(grad, mask, penalty):
    scaled = mask * jnp.abs(grad) / penalty[:, None]
    return jnp.max(scaled.reshape(grad.shape[0], -1, 128), axis=2)


def reference(genotypes, expression, coef_start, penalty, step_size, window_start, window_end, active_blocks):
    column = jnp.arange(WIDTH, dtype=jnp.int32)

    def one_group(group):
        base = group * V_DEV - HALO
        first = jnp.clip(base, 0, VARIANTS - WIDTH).astype(jnp.int32)
        shift = (base - first).astype(jnp.int32)
        cols = lax.dynamic_slice_in_dim(genotypes, first, WIDTH, 1)
        wide = jnp.take(cols, jnp.clip(column + shift, 0, WIDTH - 1), axis=1)
        gstart = (group * G_DEV).astype(jnp.int32)
        target = lax.dynamic_slice_in_dim(expression, gstart, G_DEV, 1).astype(jnp.float32)
        coef = lax.dynamic_slice_in_dim(coef_start, gstart, G_DEV, 0)
        lam = lax.dynamic_slice_in_dim(penalty, gstart, G_DEV, 0)
        step = lax.dynamic_slice_in_dim(step_size, gstart, G_DEV, 0)
        lower = lax.dynamic_slice_in_dim(window_start, gstart, G_DEV, 0)
        upper = lax.dynamic_slice_in_dim(window_end, gstart, G_DEV, 0)
        active = lax.dynamic_slice_in_dim(active_blocks, gstart, G_DEV, 0)
        place = base + column
        inside = (place[None, :] >= lower[:, None]) & (place[None, :] < upper[:, None])
        blocks = jnp.repeat(active, 128, axis=1) > 0
        mask = jnp.where(inside & blocks, 1.0, 0.0).astype(jnp.float32)
        coef = mask * coef
        peaks = None
        for turn in range(2):
            fitted = jnp.dot(wide, coef.astype(jnp.bfloat16).T, preferred_element_type=jnp.float32)
            resid = (target - fitted).astype(jnp.bfloat16)
            grad = jnp.dot(resid.T, wide, preferred_element_type=jnp.float32) / PEOPLE
            if turn == 0:
                peaks = block_peaks(grad, mask, lam)
            coef = shrink(coef, grad, lam, step, mask)
        return coef, peaks

    coefs, peaks = lax.map(one_group, jnp.arange(N_GENOME, dtype=jnp.int32))
    return coefs.reshape(GENES, WIDTH), peaks.reshape(GENES, WB)
```

```python
import jax
import jax.numpy as jnp
from jax import lax
from jax.sharding import PartitionSpec as P

l1_share = 0.5
RING = 8

KEEP_ROWS = (((1,), (1,)), ((), ()))
OVER_ROWS = (((0,), (0,)), ((), ()))


def dot(a, b, dims):
    return lax.dot_general(a, b, dims, preferred_element_type=jnp.float32)


def along_z(block, hops):
    count = 2 * RING
    return lax.ppermute(block, "people", [(i, (i + 2 * hops) % count) for i in range(count)])


def other_side(block):
    return lax.ppermute(block, "people", [(i, i ^ 1) for i in range(2 * RING)])


def sum_to_owner(pieces, z, side):
    rows = pieces[0].shape[0] // RING
    half = rows // 2

    def part(hops):
        start = lax.rem(z + hops + RING, RING) * rows
        return jnp.concatenate(
            [lax.dynamic_slice_in_dim(piece, start, rows, 0) for piece in pieces], axis=1
        )

    def pack(value):
        return value.astype(jnp.bfloat16)

    far = part(4)
    up = along_z(pack(far[:half]), 1)
    down = along_z(pack(far[half:]), -1)
    mine = part(3)
    mine = jnp.concatenate([mine[:half] + up, mine[half:]], axis=0)
    up = along_z(pack(mine), 1)
    mine = part(-3)
    mine = jnp.concatenate([mine[:half], mine[half:] + down], axis=0)
    down = along_z(pack(mine), -1)
    for hops in (2, 1):
        up = along_z(pack(part(hops) + up), 1)
        down = along_z(pack(part(-hops) + down), -1)
    total = part(0) + up + down
    keep = lax.dynamic_slice_in_dim(total, side * half, half, 0)
    give = lax.dynamic_slice_in_dim(total, (1 - side) * half, half, 0)
    return keep + other_side(pack(give))


def gather_rows(own, z, side):
    half = own.shape[0]
    rows = 2 * half
    theirs = other_side(own)
    first = jnp.where(side == 0, own, theirs)
    second = jnp.where(side == 0, theirs, own)
    pair = jnp.concatenate([first, second], axis=0)
    out = jnp.zeros((RING * rows, own.shape[1]), own.dtype)

    def put(out, block, hops, skip=0):
        start = lax.rem(z + hops + RING, RING) * rows + skip
        return lax.dynamic_update_slice_in_dim(out, block, start, 0)

    out = put(out, pair, 0)
    up = down = pair
    for hops in (1, 2, 3):
        up, down = along_z(up, 1), along_z(down, -1)
        out = put(put(out, up, -hops), down, hops)
    up, down = along_z(up[:half], 1), along_z(down[half:], -1)
    return put(put(out, up, -4), down, 4, half)


def shrink(coef, grad, penalty, step, mask):
    moved = coef + step[:, None] * grad
    cut = step[:, None] * penalty[:, None]
    kept = jnp.sign(moved) * jnp.maximum(jnp.abs(moved) - cut * l1_share, 0.0)
    return mask * kept / (1.0 + cut * (1.0 - l1_share))


def block_peaks(grad, mask, penalty):
    scaled = mask * jnp.abs(grad) / penalty[:, None]
    return jnp.max(scaled.reshape(grad.shape[0], -1, 128), axis=2)


def mask_of(start, end, active, first, width):
    place = first + jnp.arange(width, dtype=jnp.int32)
    inside = (place[None, :] >= start[:, None]) & (place[None, :] < end[:, None])
    blocks = jnp.repeat(active, 128, axis=1) > 0
    return jnp.where(inside & blocks, 1.0, 0.0).astype(jnp.float32)


def on_device(
    genotypes, expression, coef_start, penalty, step_size, window_start, window_end, active_blocks
):
    v_local = genotypes.shape[1]
    count = lax.axis_size("people")
    total = genotypes.shape[0] * count
    genes, width = coef_start.shape
    reach = (width - v_local) // 2
    chain = [(i, i + 1) for i in range(lax.axis_size("genome") - 1)]
    back = [(target, source) for source, target in chain]
    low = lax.ppermute(genotypes[:, v_local - reach :], "genome", chain)
    high = lax.ppermute(genotypes[:, :reach], "genome", back)
    cuts = (reach, reach + v_local)

    me = lax.axis_index("people")
    z, side = me // 2, me % 2
    own = genes // count
    first = lax.axis_index("genome") * v_local - reach

    def mine(array):
        return lax.dynamic_slice_in_dim(array, me * own, own, 0)

    penalty_own, step_own = mine(penalty), mine(step_size)
    mask_own = mask_of(mine(window_start), mine(window_end), mine(active_blocks), first, width)
    coef_own = mask_own * mine(coef_start)
    mask = mask_of(window_start, window_end, active_blocks, first, width)
    coef = (mask * coef_start).astype(jnp.bfloat16)

    target = expression.astype(jnp.float32)
    peaks = None
    for turn in range(2):
        fitted = dot(genotypes, coef[:, cuts[0] : cuts[1]], KEEP_ROWS)
        fitted = fitted + dot(low, coef[:, : cuts[0]], KEEP_ROWS)
        fitted = fitted + dot(high, coef[:, cuts[1] :], KEEP_ROWS)
        resid = lax.optimization_barrier((target - fitted).astype(jnp.bfloat16))
        pieces = [dot(resid, block, OVER_ROWS) for block in (low, genotypes, high)]
        grad = sum_to_owner(pieces, z, side) / total
        if turn == 0:
            peaks = block_peaks(grad, mask_own, penalty_own)
        coef_own = shrink(coef_own, grad, penalty_own, step_own, mask_own)
        sent = coef_own.astype(jnp.bfloat16)
        if turn == 0:
            major = lax.reduce_precision(peaks, 8, 7)
            tail = jnp.concatenate([major, peaks - major], axis=1).astype(jnp.bfloat16)
            tail = jnp.pad(tail, ((0, 0), (0, 128 - tail.shape[1])))
            wide = gather_rows(jnp.concatenate([sent, tail], axis=1), z, side)
            coef, tail = wide[:, :width], wide[:, width:].astype(jnp.float32)
            blocks = peaks.shape[1]
            peaks = tail[:, :blocks] + tail[:, blocks : 2 * blocks]
        else:
            coef = gather_rows(sent, z, side).astype(jnp.float32)
    return (coef, peaks)


def solution(mesh):
    return jax.shard_map(
        on_device,
        mesh=mesh,
        in_specs=(
            P("people", "genome"),
            P("people", "genome"),
            P("genome", None),
            P("genome"),
            P("genome"),
            P("genome"),
            P("genome"),
            P("genome", None),
        ),
        out_specs=(P("genome", None), P("genome", None)),
        check_vma=False,
    )
```

```python
import jax
import jax.numpy as jnp
from jax import lax
from jax.experimental import pallas as pl
from jax.experimental.pallas import tpu as pltpu
from jax.sharding import PartitionSpec as P

l1_share = 0.5
RING = 8

TILE = 512
CUT = 256


def dot(a, b):
    return jnp.dot(a, b, preferred_element_type=jnp.float32)


def turn_kernel(*refs):
    *blocks, target, coef, grad, coef_t, resid_t = refs
    people, reach = blocks[0].shape
    coef_t[...] = coef[...].T

    @pl.loop(0, target.shape[0] // TILE)
    def _(step):
        rows = pl.ds(pl.multiple_of(step * TILE, TILE), TILE)
        fitted = dot(blocks[0][rows, :], coef_t[:reach, :])
        for i in range(1, len(blocks)):
            fitted += dot(blocks[i][rows, :], coef_t[i * reach : (i + 1) * reach, :])
        resid = (target[rows, :].astype(jnp.float32) - fitted).astype(jnp.bfloat16)
        resid_t[:, rows] = resid.T

    for i, block in enumerate(blocks):
        for j in range(0, reach, CUT):
            at = i * reach + j
            offset = coef[:, at : at + CUT].astype(jnp.float32) * people
            grad[:, at : at + CUT] = dot(resid_t[...], block[:, j : j + CUT]) + offset


def in_vmem(array):
    return pltpu.with_memory_space_constraint(array, pltpu.VMEM)


def local_grad(blocks, target, coef):
    people, genes = target.shape
    width = coef.shape[1]
    operands = [in_vmem(v) for v in (*blocks, target, coef)]
    whole = pl.BlockSpec(memory_space=pltpu.VMEM)
    return pl.pallas_call(
        turn_kernel,
        out_shape=pltpu.VMEM((genes, width), jnp.float32),
        in_specs=[whole] * len(operands),
        out_specs=whole,
        scratch_shapes=[
            pltpu.VMEM((width, genes), jnp.bfloat16),
            pltpu.VMEM((genes, people), jnp.bfloat16),
        ],
        compiler_params=pltpu.CompilerParams(vmem_limit_bytes=16 << 20),
        cost_estimate=pl.CostEstimate(
            flops=4 * people * width * genes, bytes_accessed=0, transcendentals=0
        ),
    )(*operands)


def along_z(block, hops):
    count = 2 * RING
    return lax.ppermute(block, "people", [(i, (i + 2 * hops) % count) for i in range(count)])


def other_side(block):
    return lax.ppermute(block, "people", [(i, i ^ 1) for i in range(2 * RING)])


def sum_to_owner(local, z, side):
    rows = local.shape[0] // RING
    half = rows // 2

    def part(hops):
        start = lax.rem(z + hops + RING, RING) * rows
        return lax.dynamic_slice_in_dim(local, start, rows, 0)

    def pack(value):
        return value.astype(jnp.bfloat16)

    far = part(4)
    up = along_z(pack(far[:half]), 1)
    down = along_z(pack(far[half:]), -1)
    mine = part(3)
    mine = jnp.concatenate([mine[:half] + up, mine[half:]], axis=0)
    up = along_z(pack(mine), 1)
    mine = part(-3)
    mine = jnp.concatenate([mine[:half], mine[half:] + down], axis=0)
    down = along_z(pack(mine), -1)
    for hops in (2, 1):
        up = along_z(pack(part(hops) + up), 1)
        down = along_z(pack(part(-hops) + down), -1)
    total = part(0) + up + down
    keep = lax.dynamic_slice_in_dim(total, side * half, half, 0)
    give = lax.dynamic_slice_in_dim(total, (1 - side) * half, half, 0)
    return keep + other_side(pack(give))


def gather_rows(own, z, side):
    half = own.shape[0]
    rows = 2 * half
    theirs = other_side(own)
    first = jnp.where(side == 0, own, theirs)
    second = jnp.where(side == 0, theirs, own)
    pair = jnp.concatenate([first, second], axis=0)
    out = jnp.zeros((RING * rows, own.shape[1]), own.dtype)

    def put(out, block, hops, skip=0):
        start = lax.rem(z + hops + RING, RING) * rows + skip
        return lax.dynamic_update_slice_in_dim(out, block, start, 0)

    out = put(out, pair, 0)
    up = down = pair
    for hops in (1, 2, 3):
        up, down = along_z(up, 1), along_z(down, -1)
        out = put(put(out, up, -hops), down, hops)
    up, down = along_z(up[:half], 1), along_z(down[half:], -1)
    return put(put(out, up, -4), down, 4, half)


def shrink(coef, grad, penalty, step, mask):
    moved = coef + step[:, None] * grad
    cut = step[:, None] * penalty[:, None]
    kept = jnp.sign(moved) * jnp.maximum(jnp.abs(moved) - cut * l1_share, 0.0)
    return mask * kept / (1.0 + cut * (1.0 - l1_share))


def block_peaks(grad, mask, penalty):
    scaled = mask * jnp.abs(grad) / penalty[:, None]
    return jnp.max(scaled.reshape(grad.shape[0], -1, 128), axis=2)


def mask_of(start, end, active, first, width):
    place = first + jnp.arange(width, dtype=jnp.int32)
    inside = (place[None, :] >= start[:, None]) & (place[None, :] < end[:, None])
    blocks = jnp.repeat(active, 128, axis=1) > 0
    return jnp.where(inside & blocks, 1.0, 0.0).astype(jnp.float32)


def on_device(
    genotypes, expression, coef_start, penalty, step_size, window_start, window_end, active_blocks
):
    v_local = genotypes.shape[1]
    count = lax.axis_size("people")
    total = genotypes.shape[0] * count
    genes, width = coef_start.shape
    reach = (width - v_local) // 2
    chain = [(i, i + 1) for i in range(lax.axis_size("genome") - 1)]
    back = [(target, source) for source, target in chain]
    blocks = [in_vmem(genotypes[:, i : i + reach]) for i in range(0, v_local, reach)]
    low = lax.ppermute(blocks[-1], "genome", chain)
    high = lax.ppermute(blocks[0], "genome", back)
    blocks = [low, *blocks, high]

    me = lax.axis_index("people")
    z, side = me // 2, me % 2
    own = genes // count
    first = lax.axis_index("genome") * v_local - reach

    def mine(array):
        return lax.dynamic_slice_in_dim(array, me * own, own, 0)

    penalty_own, step_own = mine(penalty), mine(step_size)
    mask_own = mask_of(mine(window_start), mine(window_end), mine(active_blocks), first, width)
    coef_own = mask_own * mine(coef_start)
    mask = mask_of(window_start, window_end, active_blocks, first, width)
    coef = (mask * coef_start).astype(jnp.bfloat16)

    peaks = None
    for turn in range(2):
        grad = sum_to_owner(local_grad(blocks, expression, coef), z, side)
        grad = grad / total - mine(coef).astype(jnp.float32)
        if turn == 0:
            peaks = block_peaks(grad, mask_own, penalty_own)
        coef_own = shrink(coef_own, grad, penalty_own, step_own, mask_own)
        sent = coef_own.astype(jnp.bfloat16)
        if turn == 0:
            major = lax.reduce_precision(peaks, 8, 7)
            tail = jnp.concatenate([major, peaks - major], axis=1).astype(jnp.bfloat16)
            tail = jnp.pad(tail, ((0, 0), (0, 128 - tail.shape[1])))
            wide = gather_rows(jnp.concatenate([sent, tail], axis=1), z, side)
            coef, tail = wide[:, :width], wide[:, width:].astype(jnp.float32)
            count = peaks.shape[1]
            peaks = tail[:, :count] + tail[:, count : 2 * count]
        else:
            coef = gather_rows(sent, z, side).astype(jnp.float32)
    return (coef, peaks)


def solution(mesh):
    return jax.shard_map(
        on_device,
        mesh=mesh,
        in_specs=(
            P("people", "genome"),
            P("people", "genome"),
            P("genome", None),
            P("genome"),
            P("genome"),
            P("genome"),
            P("genome"),
            P("genome", None),
        ),
        out_specs=(P("genome", None), P("genome", None)),
        check_vma=False,
    )
```

```python
import functools

import jax
import jax.numpy as jnp
from jax import lax
from jax.experimental import pallas as pl
from jax.experimental.pallas import tpu as pltpu
from jax.sharding import PartitionSpec as P

l1_share = 0.5
SIDE, MIRROR = 1, 14
NEAR = (0, 2, 4, 6)
GIVE = ((6,), (4, 2), (0,))
OWN = 16

TILE = 512
CUT = 256


def dot(a, b):
    return jnp.dot(a, b, preferred_element_type=jnp.float32)


def rows_of(me, hop):
    return pl.ds(pl.multiple_of((me ^ hop) * OWN, OWN), OWN)


def place(me, pieces, put):
    for k, piece in enumerate(pieces):
        hop = NEAR[k % len(NEAR)] ^ (k // len(NEAR) * SIDE)
        put(rows_of(me, hop), piece[:OWN, :])
        put(rows_of(me, hop ^ MIRROR), piece[OWN:, :])


def turn_kernel(n_blocks, n_pieces, *refs):
    where, *refs = refs
    blocks, target, refs = refs[:n_blocks], refs[n_blocks], refs[n_blocks + 1 :]
    pieces, refs = refs[:n_pieces], refs[n_pieces:]
    keep, *refs = refs
    gives, refs = refs[: len(GIVE)], refs[len(GIVE) :]
    people, reach = blocks[0].shape
    width = n_blocks * reach
    me = where[0]
    if n_pieces == 1:
        coef = pieces[0]
        grad, coef_t, resid_t = refs
    else:
        tail, grad, coef_t, resid_t, coef = refs

        def put(rows, piece):
            coef[rows, :] = piece[:, :width]
            tail[rows, :] = piece[:, width:]

        place(me, pieces, put)
    coef_t[...] = coef[...].T

    @pl.loop(0, people // TILE)
    def _(step):
        rows = pl.ds(pl.multiple_of(step * TILE, TILE), TILE)
        fitted = dot(blocks[0][rows, :], coef_t[:reach, :])
        for i in range(1, n_blocks):
            fitted += dot(blocks[i][rows, :], coef_t[i * reach : (i + 1) * reach, :])
        resid = (target[rows, :].astype(jnp.float32) - fitted).astype(jnp.bfloat16)
        resid_t[:, rows] = resid.T

    for i, block in enumerate(blocks):
        for j in range(0, reach, CUT):
            at = i * reach + j
            grad[:, at : at + CUT] = dot(resid_t[...], block[:, j : j + CUT])

    def read(hop):
        rows = rows_of(me, hop)
        return grad[rows, :] + coef[rows, :].astype(jnp.float32) * people

    for give, hops in zip(gives, GIVE):
        for n, hop in enumerate(hops):
            for k, far in enumerate((0, MIRROR)):
                at = (2 * n + k) * OWN
                give[at : at + OWN, :] = read(hop ^ SIDE ^ far).astype(jnp.bfloat16)
    for n, hop in enumerate(NEAR):
        for k, far in enumerate((0, MIRROR)):
            at = (2 * n + k) * OWN
            keep[at : at + OWN, :] = read(hop ^ far)


def output_kernel(where, *refs):
    *pieces, out = refs

    def put(rows, piece):
        out[rows, :] = piece.astype(jnp.float32)

    place(where[0], pieces, put)


def in_vmem(array):
    return pltpu.with_memory_space_constraint(array, pltpu.VMEM)


def specs(count):
    vmem = pl.BlockSpec(memory_space=pltpu.VMEM)
    return [pl.BlockSpec(memory_space=pltpu.SMEM)] + [vmem] * count


def local_grad(where, blocks, target, pieces):
    people, genes = target.shape
    reach = blocks[0].shape[1]
    width = len(blocks) * reach
    operands = [in_vmem(v) for v in (*blocks, target, *pieces)]
    outs = [pltpu.VMEM((2 * OWN * len(NEAR), width), jnp.float32)]
    outs += [pltpu.VMEM((2 * OWN * len(hops), width), jnp.bfloat16) for hops in GIVE]
    scratch = [
        pltpu.VMEM((genes, width), jnp.float32),
        pltpu.VMEM((width, genes), jnp.bfloat16),
        pltpu.VMEM((genes, people), jnp.bfloat16),
    ]
    if len(pieces) > 1:
        outs.append(pltpu.VMEM((genes, pieces[0].shape[1] - width), jnp.bfloat16))
        scratch.append(pltpu.VMEM((genes, width), jnp.bfloat16))
    return pl.pallas_call(
        functools.partial(turn_kernel, len(blocks), len(pieces)),
        out_shape=outs,
        in_specs=specs(len(operands)),
        out_specs=[pl.BlockSpec(memory_space=pltpu.VMEM)] * len(outs),
        scratch_shapes=scratch,
        compiler_params=pltpu.CompilerParams(vmem_limit_bytes=20 << 20),
        cost_estimate=pl.CostEstimate(
            flops=4 * people * width * genes, bytes_accessed=0, transcendentals=0
        ),
    )(where, *operands)


def swap(block, hop):
    count = lax.axis_size("people")
    return lax.ppermute(block, "people", [(i, i ^ hop) for i in range(count)])


def sum_to_owner(keep, gives):
    part = {}
    for hops, give in zip(GIVE, gives):
        got = swap(give, SIDE)
        for n, hop in enumerate(hops):
            at = NEAR.index(hop) * 2 * OWN
            part[hop] = keep[at : at + 2 * OWN] + got[2 * n * OWN : 2 * (n + 1) * OWN]
    total = part[0]
    for hop in (6, 4, 2):
        total = total + swap(part[hop].astype(jnp.bfloat16), hop)
    return total[:OWN] + swap(total[OWN:].astype(jnp.bfloat16), MIRROR)


def gather_rows(own):
    pair = jnp.concatenate([own, swap(own, MIRROR)], axis=0)
    got = {0: pair}
    for hop in (2, 6, 4):
        got[hop] = swap(pair, hop)
    return [got[hop] for hop in NEAR] + [swap(got[hop], SIDE) for hop in NEAR]


def shrink(coef, grad, penalty, step, mask):
    moved = coef + step[:, None] * grad
    cut = step[:, None] * penalty[:, None]
    kept = jnp.sign(moved) * jnp.maximum(jnp.abs(moved) - cut * l1_share, 0.0)
    return mask * kept / (1.0 + cut * (1.0 - l1_share))


def block_peaks(grad, mask, penalty):
    scaled = mask * jnp.abs(grad) / penalty[:, None]
    return jnp.max(scaled.reshape(grad.shape[0], -1, 128), axis=2)


def mask_of(start, end, active, first, width):
    place = first + jnp.arange(width, dtype=jnp.int32)
    inside = (place[None, :] >= start[:, None]) & (place[None, :] < end[:, None])
    blocks = jnp.repeat(active, 128, axis=1) > 0
    return jnp.where(inside & blocks, 1.0, 0.0).astype(jnp.float32)


def on_device(
    genotypes, expression, coef_start, penalty, step_size, window_start, window_end, active_blocks
):
    v_local = genotypes.shape[1]
    count = lax.axis_size("people")
    total = genotypes.shape[0] * count
    genes, width = coef_start.shape
    reach = (width - v_local) // 2
    chain = [(i, i + 1) for i in range(lax.axis_size("genome") - 1)]
    back = [(target, source) for source, target in chain]
    right = in_vmem(genotypes[:, v_local - reach :])
    right, rest = lax.optimization_barrier((right, genotypes))
    low = lax.ppermute(right, "genome", chain)
    left = in_vmem(rest[:, :reach])
    high = lax.ppermute(left, "genome", back)
    blocks = [low, left, right, high]

    me = lax.axis_index("people")
    where = me[None].astype(jnp.int32)
    first = lax.axis_index("genome") * v_local - reach

    def mine(array):
        return lax.dynamic_slice_in_dim(array, me * OWN, OWN, 0)

    penalty_own, step_own = mine(penalty), mine(step_size)
    mask_own = mask_of(mine(window_start), mine(window_end), mine(active_blocks), first, width)
    coef_own = mask_own * mine(coef_start)
    mask = mask_of(window_start, window_end, active_blocks, first, width)
    coef = (mask * coef_start).astype(jnp.bfloat16)

    keep, *gives = local_grad(where, blocks, expression, [coef])
    base = mine(coef).astype(jnp.float32)
    grad = sum_to_owner(keep, gives) / total - base
    peaks = block_peaks(grad, mask_own, penalty_own)
    coef_own = shrink(coef_own, grad, penalty_own, step_own, mask_own)
    sent = coef_own.astype(jnp.bfloat16)
    major = lax.reduce_precision(peaks, 8, 7)
    tail = jnp.concatenate([major, peaks - major], axis=1).astype(jnp.bfloat16)
    tail = jnp.pad(tail, ((0, 0), (0, 128 - tail.shape[1])))
    pieces = gather_rows(jnp.concatenate([sent, tail], axis=1))

    keep, *gives, tail = local_grad(where, blocks, expression, pieces)
    tail = tail.astype(jnp.float32)
    n_peaks = peaks.shape[1]
    peaks = tail[:, :n_peaks] + tail[:, n_peaks : 2 * n_peaks]
    grad = sum_to_owner(keep, gives) / total - sent.astype(jnp.float32)
    coef_own = shrink(coef_own, grad, penalty_own, step_own, mask_own)
    pieces = gather_rows(coef_own.astype(jnp.bfloat16))
    coef = pl.pallas_call(
        output_kernel,
        out_shape=jax.ShapeDtypeStruct((genes, width), jnp.float32),
        in_specs=specs(len(pieces)),
        out_specs=pl.BlockSpec(memory_space=pltpu.VMEM),
        compiler_params=pltpu.CompilerParams(vmem_limit_bytes=8 << 20),
    )(where, *[in_vmem(piece) for piece in pieces])
    return (coef, peaks)


def solution(mesh):
    return jax.shard_map(
        on_device,
        mesh=mesh,
        in_specs=(
            P("people", "genome"),
            P("people", "genome"),
            P("genome", None),
            P("genome"),
            P("genome"),
            P("genome"),
            P("genome"),
            P("genome", None),
        ),
        out_specs=(P("genome", None), P("genome", None)),
        check_vma=False,
    )
```

```python
import functools

import jax
import jax.numpy as jnp
from jax import lax
from jax.experimental import pallas as pl
from jax.experimental.pallas import tpu as pltpu
from jax.sharding import PartitionSpec as P

l1_share = 0.5
SIDE, MIRROR = 1, 14
NEAR = (0, 2, 4, 6)
GIVE = ((6,), (4, 2), (0,))
OWN = 16
PEOPLE = 16
LANES = 128
START, END, PENALTY, STEP = 16, 17, 18, 19

TILE = 768
PARTS = (2304, 768)
CUT = 256


def dot(a, b):
    return jnp.dot(a, b, preferred_element_type=jnp.float32)


def rows_of(me, hop):
    return pl.ds(pl.multiple_of((me ^ hop) * OWN, OWN), OWN)


def dot_t(a, b):
    return lax.dot_general(a, b, (((1,), (1,)), ((), ())), preferred_element_type=jnp.float32)


def person(where):
    return where[0] % PEOPLE


def place(me, pieces, put):
    for k, piece in enumerate(pieces):
        hop = NEAR[k % len(NEAR)] ^ (k // len(NEAR) * SIDE)
        put(rows_of(me, hop), piece[:OWN, :])
        put(rows_of(me, hop ^ MIRROR), piece[OWN:, :])


def turn_kernel(parts, n_pieces, add, pack, *refs):
    where, *refs = refs
    blocks, refs = refs[: 4 * len(parts)], refs[4 * len(parts) :]
    target, *refs = refs
    pieces, refs = refs[:n_pieces], refs[n_pieces:]
    if add:
        prior, *refs = refs
    reach = blocks[0].shape[1]
    width = 4 * reach
    me = person(where)
    if pack:
        keep, *refs = refs
        gives, refs = refs[: len(GIVE)], refs[len(GIVE) :]
    if n_pieces > 1:
        peaks, *refs = refs
    grad, resid_t, *refs = refs
    if n_pieces > 1:
        coef, tail = refs

        def put(rows, piece):
            coef[rows, :] = piece[:, :width]
            tail[rows, :] = piece[:, width:]

        place(me, pieces, put)
        count = peaks.shape[0]
        flat = tail[...].astype(jnp.float32).T
        peaks[...] = flat[:count, :] + flat[count : 2 * count, :]
    else:
        (coef,) = pieces

    done = 0
    for k, (first, count) in enumerate(parts):
        for step in range(0, count, TILE):
            rows = pl.ds(step, TILE)
            fitted = 0.0
            for i in range(4):
                weights = coef[:, i * reach : (i + 1) * reach]
                fitted += dot_t(blocks[4 * k + i][rows, :], weights)
            goal = target[pl.ds(first + step, TILE), :].astype(jnp.float32)
            resid_t[:, pl.ds(done, TILE)] = (goal - fitted).astype(jnp.bfloat16).T
            done += TILE

    for i in range(4):
        for j in range(0, reach, CUT):
            at = i * reach + j
            total = prior[:, at : at + CUT] if add else 0.0
            done = 0
            for k, (first, count) in enumerate(parts):
                block = blocks[4 * k + i]
                total += dot(resid_t[:, pl.ds(done, count)], block[:, j : j + CUT])
                done += count
            grad[:, at : at + CUT] = total
    if not pack:
        return

    def read(hop):
        rows = rows_of(me, hop)
        return grad[rows, :] + coef[rows, :].astype(jnp.float32) * target.shape[0]

    for give, hops in zip(gives, GIVE):
        for n, hop in enumerate(hops):
            for k, far in enumerate((0, MIRROR)):
                at = (2 * n + k) * OWN
                give[at : at + OWN, :] = read(hop ^ SIDE ^ far).astype(jnp.bfloat16)
    for n, hop in enumerate(NEAR):
        for k, far in enumerate((0, MIRROR)):
            at = (2 * n + k) * OWN
            keep[at : at + OWN, :] = read(hop ^ far)


def block_mask(where, table, block, reach):
    rows = table.shape[0]
    first = where[0] // PEOPLE * (2 * reach) - reach + block * LANES
    column = lax.broadcasted_iota(jnp.int32, (rows, LANES), 1) + first
    column = column.astype(jnp.float32)
    inside = (column >= table[:, START : START + 1]) & (column < table[:, END : END + 1])
    return jnp.where(inside & (table[:, block : block + 1] > 0), 1.0, 0.0)


def start_kernel(where, active, *refs):
    *vectors, coef_start, by_gene, coef, coef_own, table = refs
    table[...] = jnp.zeros(table.shape, jnp.float32)
    table[: active.shape[0], :] = active[...].astype(jnp.float32)
    for row, vector in zip((START, END, PENALTY, STEP), vectors):
        table[row : row + 1, :] = vector[...].astype(jnp.float32)
    by_gene[...] = table[...].T
    own = rows_of(person(where), 0)
    width = coef.shape[1]
    for block in range(width // LANES):
        cols = slice(block * LANES, (block + 1) * LANES)
        mask = block_mask(where, by_gene[...], block, width // 4)
        coef[:, cols] = (mask * coef_start[:, cols]).astype(jnp.bfloat16)
        mask = block_mask(where, by_gene[own, :], block, width // 4)
        coef_own[:, cols] = mask * coef_start[own, cols]


def update_kernel(total, first, where, by_gene, near, far, coef_own, base, *refs):
    own = rows_of(person(where), 0)
    table = by_gene[own, :]
    width = coef_own.shape[1]
    penalty, step = table[:, PENALTY : PENALTY + 1], table[:, STEP : STEP + 1]
    cut = step * penalty
    lane = lax.broadcasted_iota(jnp.int32, (OWN, LANES), 1)
    high = low = jnp.zeros((OWN, LANES), jnp.float32)
    for block in range(width // LANES):
        cols = slice(block * LANES, (block + 1) * LANES)
        mask = block_mask(where, table, block, width // 4)
        used = base[own, cols] if first else base[:, cols]
        grad = (near[:OWN, cols] + far[:, cols].astype(jnp.float32)) / total - used.astype(jnp.float32)
        moved = coef_own[:, cols] + step * grad
        size = jnp.maximum(jnp.abs(moved) - cut * l1_share, 0.0)
        kept = mask * jnp.where(moved < 0, -size, size) / (1.0 + cut * (1.0 - l1_share))
        if first:
            refs[0][:, cols] = kept
            peak = jnp.max(mask * jnp.abs(grad) / penalty, axis=1, keepdims=True)
            rounded = peak.astype(jnp.bfloat16).astype(jnp.float32)
            high = jnp.where(lane == block, rounded, high)
            low = jnp.where(lane == block + width // LANES, peak - rounded, low)
        refs[-1][:, cols] = kept.astype(jnp.bfloat16)
    if first:
        refs[-1][:, width:] = (high + low).astype(jnp.bfloat16)


def output_kernel(where, *refs):
    *pieces, out = refs

    def put(rows, piece):
        out[rows, :] = piece.astype(jnp.float32)

    place(person(where), pieces, put)


def in_vmem(array):
    return pltpu.with_memory_space_constraint(array, pltpu.VMEM)


def specs(count):
    vmem = pl.BlockSpec(memory_space=pltpu.VMEM)
    return [pl.BlockSpec(memory_space=pltpu.SMEM)] + [vmem] * count


def split(genotypes, reach):
    out, first = [], 0
    for count in PARTS:
        for column in (reach, 0):
            piece = genotypes[first : first + count, column : column + reach]
            piece, genotypes = lax.optimization_barrier((piece, genotypes))
            out.append(in_vmem(piece))
        first += count
    return out


def local_grad(where, chosen, blocks, target, pieces, prior=None, pack=True):
    genes = target.shape[1]
    reach = blocks[0][0].shape[1]
    width = 4 * reach
    parts = [(sum(PARTS[:k]), PARTS[k]) for k in chosen]
    people = sum(count for _, count in parts)
    given = [block for k in chosen for block in blocks[k]]
    operands = [*given, target, *pieces] + ([] if prior is None else [prior])
    operands = [in_vmem(v) for v in operands]
    local = pltpu.VMEM((genes, width), jnp.float32)
    outs, scratch = [], [pltpu.VMEM((genes, people), jnp.bfloat16)]
    if pack:
        outs.append(pltpu.VMEM((2 * OWN * len(NEAR), width), jnp.float32))
        outs += [pltpu.VMEM((2 * OWN * len(hops), width), jnp.bfloat16) for hops in GIVE]
        scratch = [local, *scratch]
    else:
        outs.append(local)
    if len(pieces) > 1:
        outs.append(pltpu.VMEM((width // LANES, genes), jnp.float32))
        scratch.append(pltpu.VMEM((genes, width), jnp.bfloat16))
        scratch.append(pltpu.VMEM((genes, LANES), jnp.bfloat16))
    return pl.pallas_call(
        functools.partial(turn_kernel, parts, len(pieces), prior is not None, pack),
        out_shape=outs,
        in_specs=specs(len(operands)),
        out_specs=[pl.BlockSpec(memory_space=pltpu.VMEM)] * len(outs),
        scratch_shapes=scratch,
        compiler_params=pltpu.CompilerParams(vmem_limit_bytes=20 << 20),
        cost_estimate=pl.CostEstimate(
            flops=4 * people * width * genes, bytes_accessed=0, transcendentals=0
        ),
    )(where, *operands)


def small_call(kernel, where, operands, outs, scratch=()):
    return pl.pallas_call(
        kernel,
        out_shape=[pltpu.VMEM(shape, dtype) for shape, dtype in outs],
        in_specs=specs(len(operands)),
        out_specs=[pl.BlockSpec(memory_space=pltpu.VMEM)] * len(outs),
        scratch_shapes=list(scratch),
        compiler_params=pltpu.CompilerParams(vmem_limit_bytes=8 << 20),
    )(where, *[in_vmem(v) for v in operands])


def swap(block, hop):
    count = lax.axis_size("people")
    return lax.ppermute(block, "people", [(i, i ^ hop) for i in range(count)])


def sum_to_owner(keep, gives):
    part = {}
    for hops, give in zip(GIVE, gives):
        got = swap(give, SIDE)
        for n, hop in enumerate(hops):
            at = NEAR.index(hop) * 2 * OWN
            part[hop] = keep[at : at + 2 * OWN] + got[2 * n * OWN : 2 * (n + 1) * OWN]
    total = part[0]
    for hop in (6, 4, 2):
        total = total + swap(part[hop].astype(jnp.bfloat16), hop)
    return total, swap(total[OWN:].astype(jnp.bfloat16), MIRROR)


def gather_rows(own):
    pair = jnp.concatenate([own, swap(own, MIRROR)], axis=0)
    got = {0: pair}
    for hop in (2, 6, 4):
        got[hop] = swap(pair, hop)
    return [got[hop] for hop in NEAR] + [swap(got[hop], SIDE) for hop in NEAR]


def on_device(
    genotypes, expression, coef_start, penalty, step_size, window_start, window_end, active_blocks
):
    v_local = genotypes.shape[1]
    total = genotypes.shape[0] * lax.axis_size("people")
    genes, width = coef_start.shape
    reach = (width - v_local) // 2
    chain = [(i, i + 1) for i in range(lax.axis_size("genome") - 1)]
    back = [(target, source) for source, target in chain]
    where = lax.axis_index(("genome", "people")).astype(jnp.int32)[None]
    vectors = [v[None] for v in (window_start, window_end, penalty, step_size)]
    by_gene, coef, coef_own = small_call(
        start_kernel,
        where,
        [active_blocks.T, *vectors, coef_start],
        [((genes, LANES), jnp.float32), ((genes, width), jnp.bfloat16), ((OWN, width), jnp.float32)],
        [pltpu.VMEM((LANES, genes), jnp.float32)],
    )

    halves = split(genotypes, reach)
    blocks = []
    for k in range(len(PARTS)):
        right, left = halves[2 * k], halves[2 * k + 1]
        before = (blocks[0][0], blocks[0][3], coef) if k else (where,)
        right, left, *_ = lax.optimization_barrier((right, left, *before))
        low = lax.ppermute(right, "genome", chain)
        high = lax.ppermute(left, "genome", back)
        blocks.append((low, left, right, high))

    (prior,) = local_grad(where, (0,), blocks, expression, [coef], pack=False)
    keep, *gives = local_grad(where, (1,), blocks, expression, [coef], prior)
    near, far = sum_to_owner(keep, gives)
    coef_own, sent = small_call(
        functools.partial(update_kernel, total, True),
        where,
        [by_gene, near, far, coef_own, coef],
        [((OWN, width), jnp.float32), ((OWN, width + LANES), jnp.bfloat16)],
    )
    pieces = gather_rows(sent)

    keep, *gives, peaks = local_grad(where, (0, 1), blocks, expression, pieces)
    near, far = sum_to_owner(keep, gives)
    (last,) = small_call(
        functools.partial(update_kernel, total, False),
        where,
        [by_gene, near, far, coef_own, sent],
        [((OWN, width), jnp.bfloat16)],
    )
    pieces = gather_rows(last)
    coef = pl.pallas_call(
        output_kernel,
        out_shape=jax.ShapeDtypeStruct((genes, width), jnp.float32),
        in_specs=specs(len(pieces)),
        out_specs=pl.BlockSpec(memory_space=pltpu.VMEM),
        compiler_params=pltpu.CompilerParams(vmem_limit_bytes=8 << 20),
    )(where, *[in_vmem(piece) for piece in pieces])
    return (coef, peaks.T)


def solution(mesh):
    return jax.shard_map(
        on_device,
        mesh=mesh,
        in_specs=(
            P("people", "genome"),
            P("people", "genome"),
            P("genome", None),
            P("genome"),
            P("genome"),
            P("genome"),
            P("genome"),
            P("genome", None),
        ),
        out_specs=(P("genome", None), P("genome", None)),
        check_vma=False,
    )
```

```python
import functools

import jax
import jax.numpy as jnp
from jax import lax
from jax.experimental import pallas as pl
from jax.experimental.pallas import tpu as pltpu
from jax.sharding import PartitionSpec as P

l1_share = 0.5
SIDE, MIRROR = 1, 14
NEAR = (0, 2, 4, 6)
GIVE = ((6,), (4, 2), (0,))
OWN = 16
PEOPLE = 16
LANES = 128
START, END, PENALTY, STEP = 16, 17, 18, 19

TILE = 768
COPIES = 4
CUT = 256


def dot(a, b):
    return jnp.dot(a, b, preferred_element_type=jnp.float32)


def rows_of(me, hop):
    return pl.ds(pl.multiple_of((me ^ hop) * OWN, OWN), OWN)


def dot_t(a, b):
    return lax.dot_general(a, b, (((1,), (1,)), ((), ())), preferred_element_type=jnp.float32)


def person(where):
    return where[0] % PEOPLE


def place(me, pieces, put):
    for k, piece in enumerate(pieces):
        hop = NEAR[k % len(NEAR)] ^ (k // len(NEAR) * SIDE)
        put(rows_of(me, hop), piece[:OWN, :])
        put(rows_of(me, hop ^ MIRROR), piece[OWN:, :])


def cut_kernel(where, whole, away, beside, sems):
    people, reach = away.shape
    count = people // COPIES
    core = where[0] // PEOPLE % 2
    copies = []
    for n, (out, half) in enumerate(((away, core), (beside, 1 - core))):
        cols = pl.ds(pl.multiple_of(half * reach, reach), reach)
        for k in range(COPIES):
            rows = pl.ds(k * count, count)
            sem = sems.at[n * COPIES + k]
            copies.append(pltpu.make_async_copy(whole.at[rows, cols], out.at[rows, :], sem))
    for copy in copies:
        copy.start()
    for copy in copies:
        copy.wait()


def column_of(where, block, reach):
    core = where[0] // PEOPLE % 2
    return pl.multiple_of((block + core * (3 - 2 * block)) * reach, reach)


def fit(where, rows, blocks, coef):
    fitted = 0.0
    for i, block in blocks.items():
        reach = block.shape[1]
        fitted += dot_t(block[rows, :], coef[:, pl.ds(column_of(where, i, reach), reach)])
    return fitted


def early_kernel(where, second, third, fourth, target, coef, part):
    blocks = {1: second, 2: third, 3: fourth}
    for step in range(0, target.shape[0], TILE):
        rows = pl.ds(step, TILE)
        part[rows, :] = target[rows, :].astype(jnp.float32) - fit(where, rows, blocks, coef)


def turn_kernel(n_pieces, *refs):
    where, *refs = refs
    blocks, refs = refs[:4], refs[4:]
    target, *refs = refs
    pieces, refs = refs[:n_pieces], refs[n_pieces:]
    keep, *refs = refs
    gives, refs = refs[: len(GIVE)], refs[len(GIVE) :]
    reach = blocks[0].shape[1]
    width = 4 * reach
    me = person(where)
    if n_pieces > 1:
        peaks, grad, resid_t, coef, tail = refs

        def put(rows, piece):
            coef[rows, :] = piece[:, :width]
            tail[rows, :] = piece[:, width:]

        place(me, pieces, put)
        count = peaks.shape[0]
        flat = tail[...].astype(jnp.float32).T
        peaks[...] = flat[:count, :] + flat[count : 2 * count, :]
    else:
        (coef,) = pieces
        grad, resid_t = refs

    last = {0: blocks[0]} if n_pieces == 1 else dict(enumerate(blocks))
    for step in range(0, target.shape[0], TILE):
        rows = pl.ds(step, TILE)
        resid = target[rows, :].astype(jnp.float32) - fit(where, rows, last, coef)
        resid_t[:, rows] = resid.astype(jnp.bfloat16).T

    for i, block in enumerate(blocks):
        for j in range(0, reach, CUT):
            cols = pl.ds(pl.multiple_of(column_of(where, i, reach) + j, CUT), CUT)
            grad[:, cols] = dot(resid_t[...], block[:, j : j + CUT])

    def read(hop):
        rows = rows_of(me, hop)
        return grad[rows, :] + coef[rows, :].astype(jnp.float32) * target.shape[0]

    for give, hops in zip(gives, GIVE):
        for n, hop in enumerate(hops):
            for k, far in enumerate((0, MIRROR)):
                at = (2 * n + k) * OWN
                give[at : at + OWN, :] = read(hop ^ SIDE ^ far).astype(jnp.bfloat16)
    for n, hop in enumerate(NEAR):
        for k, far in enumerate((0, MIRROR)):
            at = (2 * n + k) * OWN
            keep[at : at + OWN, :] = read(hop ^ far)


def block_mask(where, table, block, reach):
    rows = table.shape[0]
    first = where[0] // PEOPLE * (2 * reach) - reach + block * LANES
    column = lax.broadcasted_iota(jnp.int32, (rows, LANES), 1) + first
    column = column.astype(jnp.float32)
    inside = (column >= table[:, START : START + 1]) & (column < table[:, END : END + 1])
    return jnp.where(inside & (table[:, block : block + 1] > 0), 1.0, 0.0)


def start_kernel(where, active, *refs):
    *vectors, coef_start, by_gene, coef, coef_own, table = refs
    table[...] = jnp.zeros(table.shape, jnp.float32)
    table[: active.shape[0], :] = active[...].astype(jnp.float32)
    for row, vector in zip((START, END, PENALTY, STEP), vectors):
        table[row : row + 1, :] = vector[...].astype(jnp.float32)
    by_gene[...] = table[...].T
    own = rows_of(person(where), 0)
    width = coef.shape[1]
    for block in range(width // LANES):
        cols = slice(block * LANES, (block + 1) * LANES)
        mask = block_mask(where, by_gene[...], block, width // 4)
        coef[:, cols] = (mask * coef_start[:, cols]).astype(jnp.bfloat16)
        mask = block_mask(where, by_gene[own, :], block, width // 4)
        coef_own[:, cols] = mask * coef_start[own, cols]


def update_kernel(total, first, where, by_gene, near, far, coef_own, base, *refs):
    own = rows_of(person(where), 0)
    table = by_gene[own, :]
    width = coef_own.shape[1]
    penalty, step = table[:, PENALTY : PENALTY + 1], table[:, STEP : STEP + 1]
    cut = step * penalty
    lane = lax.broadcasted_iota(jnp.int32, (OWN, LANES), 1)
    high = low = jnp.zeros((OWN, LANES), jnp.float32)
    for block in range(width // LANES):
        cols = slice(block * LANES, (block + 1) * LANES)
        mask = block_mask(where, table, block, width // 4)
        used = base[own, cols] if first else base[:, cols]
        grad = (near[:OWN, cols] + far[:, cols].astype(jnp.float32)) / total - used.astype(jnp.float32)
        moved = coef_own[:, cols] + step * grad
        size = jnp.maximum(jnp.abs(moved) - cut * l1_share, 0.0)
        kept = mask * jnp.where(moved < 0, -size, size) / (1.0 + cut * (1.0 - l1_share))
        if first:
            refs[0][:, cols] = kept
            peak = jnp.max(mask * jnp.abs(grad) / penalty, axis=1, keepdims=True)
            rounded = peak.astype(jnp.bfloat16).astype(jnp.float32)
            high = jnp.where(lane == block, rounded, high)
            low = jnp.where(lane == block + width // LANES, peak - rounded, low)
        refs[-1][:, cols] = kept.astype(jnp.bfloat16)
    if first:
        refs[-1][:, width:] = (high + low).astype(jnp.bfloat16)


def output_kernel(where, *refs):
    *pieces, out = refs

    def put(rows, piece):
        out[rows, :] = piece.astype(jnp.float32)

    place(person(where), pieces, put)


def in_vmem(array):
    return pltpu.with_memory_space_constraint(array, pltpu.VMEM)


def specs(count):
    vmem = pl.BlockSpec(memory_space=pltpu.VMEM)
    return [pl.BlockSpec(memory_space=pltpu.SMEM)] + [vmem] * count


def cut_columns(where, genotypes, reach):
    half = pltpu.VMEM((genotypes.shape[0], reach), genotypes.dtype)
    return pl.pallas_call(
        cut_kernel,
        out_shape=[half, half],
        in_specs=[pl.BlockSpec(memory_space=pltpu.SMEM), pl.BlockSpec(memory_space=pltpu.HBM)],
        out_specs=[pl.BlockSpec(memory_space=pltpu.VMEM)] * 2,
        scratch_shapes=[pltpu.SemaphoreType.DMA((2 * COPIES,))],
        compiler_params=pltpu.CompilerParams(vmem_limit_bytes=8 << 20),
    )(where, pltpu.with_memory_space_constraint(genotypes, pltpu.HBM))


def cost(people, blocks, products):
    flops = 2 * products * people * blocks.shape[0] * blocks.shape[1]
    return pl.CostEstimate(flops=flops, bytes_accessed=0, transcendentals=0)


def early_part(where, blocks, target, coef):
    operands = [in_vmem(v) for v in (*blocks, target, coef)]
    return pl.pallas_call(
        early_kernel,
        out_shape=pltpu.VMEM(target.shape, jnp.float32),
        in_specs=specs(len(operands)),
        out_specs=pl.BlockSpec(memory_space=pltpu.VMEM),
        compiler_params=pltpu.CompilerParams(vmem_limit_bytes=8 << 20),
        cost_estimate=pl.CostEstimate(flops=0, bytes_accessed=0, transcendentals=0),
    )(where, *operands)


def local_grad(where, blocks, target, pieces):
    people, genes = target.shape
    width = 4 * blocks[0].shape[1]
    operands = [in_vmem(v) for v in (*blocks, target, *pieces)]
    outs = [pltpu.VMEM((2 * OWN * len(NEAR), width), jnp.float32)]
    outs += [pltpu.VMEM((2 * OWN * len(hops), width), jnp.bfloat16) for hops in GIVE]
    scratch = [pltpu.VMEM((genes, width), jnp.float32), pltpu.VMEM((genes, people), jnp.bfloat16)]
    if len(pieces) > 1:
        outs.append(pltpu.VMEM((width // LANES, genes), jnp.float32))
        scratch.append(pltpu.VMEM((genes, width), jnp.bfloat16))
        scratch.append(pltpu.VMEM((genes, LANES), jnp.bfloat16))
    return pl.pallas_call(
        functools.partial(turn_kernel, len(pieces)),
        out_shape=outs,
        in_specs=specs(len(operands)),
        out_specs=[pl.BlockSpec(memory_space=pltpu.VMEM)] * len(outs),
        scratch_shapes=scratch,
        compiler_params=pltpu.CompilerParams(vmem_limit_bytes=20 << 20),
        cost_estimate=cost(people, jax.ShapeDtypeStruct((genes, width), jnp.bfloat16), 2),
    )(where, *operands)


def small_call(kernel, where, operands, outs, scratch=()):
    return pl.pallas_call(
        kernel,
        out_shape=[pltpu.VMEM(shape, dtype) for shape, dtype in outs],
        in_specs=specs(len(operands)),
        out_specs=[pl.BlockSpec(memory_space=pltpu.VMEM)] * len(outs),
        scratch_shapes=list(scratch),
        compiler_params=pltpu.CompilerParams(vmem_limit_bytes=8 << 20),
    )(where, *[in_vmem(v) for v in operands])


def swap(block, hop):
    count = lax.axis_size("people")
    return lax.ppermute(block, "people", [(i, i ^ hop) for i in range(count)])


def sum_to_owner(keep, gives):
    part = {}
    for hops, give in zip(GIVE, gives):
        got = swap(give, SIDE)
        for n, hop in enumerate(hops):
            at = NEAR.index(hop) * 2 * OWN
            part[hop] = keep[at : at + 2 * OWN] + got[2 * n * OWN : 2 * (n + 1) * OWN]
    total = part[0]
    for hop in (6, 4, 2):
        total = total + swap(part[hop].astype(jnp.bfloat16), hop)
    return total, swap(total[OWN:].astype(jnp.bfloat16), MIRROR)


def gather_rows(own):
    pair = jnp.concatenate([own, swap(own, MIRROR)], axis=0)
    got = {0: pair}
    for hop in (2, 6, 4):
        got[hop] = swap(pair, hop)
    return [got[hop] for hop in NEAR] + [swap(got[hop], SIDE) for hop in NEAR]


def on_device(
    genotypes, expression, coef_start, penalty, step_size, window_start, window_end, active_blocks
):
    v_local = genotypes.shape[1]
    total = genotypes.shape[0] * lax.axis_size("people")
    genes, width = coef_start.shape
    reach = (width - v_local) // 2
    count = lax.axis_size("genome")
    sibling = [(i, i ^ 1) for i in range(count)]
    beyond = [(i, i + 1 if i % 2 else i - 1) for i in range(count)]
    beyond = [(source, target) for source, target in beyond if 0 <= target < count]
    where = lax.axis_index(("genome", "people")).astype(jnp.int32)[None]
    vectors = [v[None] for v in (window_start, window_end, penalty, step_size)]
    by_gene, coef, coef_own = small_call(
        start_kernel,
        where,
        [active_blocks.T, *vectors, coef_start],
        [((genes, LANES), jnp.float32), ((genes, width), jnp.bfloat16), ((OWN, width), jnp.float32)],
        [pltpu.VMEM((LANES, genes), jnp.float32)],
    )

    away, beside = cut_columns(where, genotypes, reach)
    slow = lax.ppermute(away, "genome", beyond)
    fast = lax.ppermute(beside, "genome", sibling)
    blocks = [slow, away, beside, fast]
    part = early_part(where, blocks[1:], expression, coef)
    keep, *gives = local_grad(where, blocks, part, [coef])
    near, far = sum_to_owner(keep, gives)
    coef_own, sent = small_call(
        functools.partial(update_kernel, total, True),
        where,
        [by_gene, near, far, coef_own, coef],
        [((OWN, width), jnp.float32), ((OWN, width + LANES), jnp.bfloat16)],
    )
    pieces = gather_rows(sent)

    keep, *gives, peaks = local_grad(where, blocks, expression, pieces)
    near, far = sum_to_owner(keep, gives)
    (last,) = small_call(
        functools.partial(update_kernel, total, False),
        where,
        [by_gene, near, far, coef_own, sent],
        [((OWN, width), jnp.bfloat16)],
    )
    pieces = gather_rows(last)
    coef = pl.pallas_call(
        output_kernel,
        out_shape=jax.ShapeDtypeStruct((genes, width), jnp.float32),
        in_specs=specs(len(pieces)),
        out_specs=pl.BlockSpec(memory_space=pltpu.VMEM),
        compiler_params=pltpu.CompilerParams(vmem_limit_bytes=8 << 20),
    )(where, *[in_vmem(piece) for piece in pieces])
    return (coef, peaks.T)


def solution(mesh):
    return jax.shard_map(
        on_device,
        mesh=mesh,
        in_specs=(
            P("people", "genome"),
            P("people", "genome"),
            P("genome", None),
            P("genome"),
            P("genome"),
            P("genome"),
            P("genome"),
            P("genome", None),
        ),
        out_specs=(P("genome", None), P("genome", None)),
        check_vma=False,
    )
```

```python
import functools

import jax
import jax.numpy as jnp
from jax import lax
from jax.experimental import pallas as pl
from jax.experimental.pallas import tpu as pltpu
from jax.sharding import PartitionSpec as P

l1_share = 0.5
SIDE, MIRROR = 1, 14
NEAR = (0, 2, 4, 6)
GIVE = ((6,), (4, 2), (0,))
OWN = 16
PEOPLE = 16
LANES = 128
START, END, PENALTY, STEP = 16, 17, 18, 19

TILE = 768
COPIES = 4
CUT = 256


def dot(a, b):
    return jnp.dot(a, b, preferred_element_type=jnp.float32)


def rows_of(me, hop):
    return pl.ds(pl.multiple_of((me ^ hop) * OWN, OWN), OWN)


def dot_t(a, b):
    return lax.dot_general(a, b, (((1,), (1,)), ((), ())), preferred_element_type=jnp.float32)


def person(where):
    return where[0] % PEOPLE


def place(me, pieces, put):
    for k, piece in enumerate(pieces):
        hop = NEAR[k % len(NEAR)] ^ (k // len(NEAR) * SIDE)
        put(rows_of(me, hop), piece[:OWN, :])
        put(rows_of(me, hop ^ MIRROR), piece[OWN:, :])


def cut_kernel(where, whole, away, beside, sems):
    people, reach = away.shape
    count = people // COPIES
    core = where[0] // PEOPLE % 2
    copies = []
    for n, (out, half) in enumerate(((away, core), (beside, 1 - core))):
        cols = pl.ds(pl.multiple_of(half * reach, reach), reach)
        for k in range(COPIES):
            rows = pl.ds(k * count, count)
            sem = sems.at[n * COPIES + k]
            copies.append(pltpu.make_async_copy(whole.at[rows, cols], out.at[rows, :], sem))
    for copy in copies:
        copy.start()
    for copy in copies:
        copy.wait()


def column_of(where, block, reach):
    core = where[0] // PEOPLE % 2
    return pl.multiple_of((block + core * (3 - 2 * block)) * reach, reach)


def fit(where, rows, blocks, coef):
    fitted = 0.0
    for i, block in blocks.items():
        reach = block.shape[1]
        fitted += dot_t(block[rows, :], coef[:, pl.ds(column_of(where, i, reach), reach)])
    return fitted


def early_kernel(where, second, third, fourth, target, coef, part):
    blocks = {1: second, 2: third, 3: fourth}
    for step in range(0, target.shape[0], TILE):
        rows = pl.ds(step, TILE)
        part[rows, :] = target[rows, :].astype(jnp.float32) - fit(where, rows, blocks, coef)


def turn_kernel(n_pieces, *refs):
    where, *refs = refs
    blocks, refs = refs[:4], refs[4:]
    target, *refs = refs
    pieces, refs = refs[:n_pieces], refs[n_pieces:]
    keep, *refs = refs
    gives, refs = refs[: len(GIVE)], refs[len(GIVE) :]
    reach = blocks[0].shape[1]
    width = 4 * reach
    me = person(where)
    if n_pieces > 1:
        peaks, grad, resid_t, coef, tail = refs

        def put(rows, piece):
            coef[rows, :] = piece[:, :width]
            tail[rows, :] = piece[:, width:]

        place(me, pieces, put)
        count = peaks.shape[0]
        flat = tail[...].astype(jnp.float32).T
        peaks[...] = flat[:count, :] + flat[count : 2 * count, :]
    else:
        (coef,) = pieces
        grad, resid_t = refs

    last = {0: blocks[0]} if n_pieces == 1 else dict(enumerate(blocks))
    for step in range(0, target.shape[0], TILE):
        rows = pl.ds(step, TILE)
        resid = target[rows, :].astype(jnp.float32) - fit(where, rows, last, coef)
        resid_t[:, rows] = resid.astype(jnp.bfloat16).T

    for i, block in enumerate(blocks):
        for j in range(0, reach, CUT):
            cols = pl.ds(pl.multiple_of(column_of(where, i, reach) + j, CUT), CUT)
            grad[:, cols] = dot(resid_t[...], block[:, j : j + CUT])

    def read(hop):
        rows = rows_of(me, hop)
        return grad[rows, :] + coef[rows, :].astype(jnp.float32) * target.shape[0]

    for give, hops in zip(gives, GIVE):
        for n, hop in enumerate(hops):
            for k, far in enumerate((0, MIRROR)):
                at = (2 * n + k) * OWN
                give[at : at + OWN, :] = read(hop ^ SIDE ^ far).astype(jnp.bfloat16)
    for n, hop in enumerate(NEAR):
        for k, far in enumerate((0, MIRROR)):
            at = (2 * n + k) * OWN
            keep[at : at + OWN, :] = read(hop ^ far)


def block_mask(where, table, block, reach):
    rows = table.shape[0]
    first = where[0] // PEOPLE * (2 * reach) - reach + block * LANES
    column = lax.broadcasted_iota(jnp.int32, (rows, LANES), 1) + first
    column = column.astype(jnp.float32)
    inside = (column >= table[:, START : START + 1]) & (column < table[:, END : END + 1])
    return jnp.where(inside & (table[:, block : block + 1] > 0), 1.0, 0.0)


def start_kernel(where, active, *refs):
    *vectors, coef_start, by_gene, coef, coef_own, table = refs
    table[...] = jnp.zeros(table.shape, jnp.float32)
    table[: active.shape[0], :] = active[...].astype(jnp.float32)
    for row, vector in zip((START, END, PENALTY, STEP), vectors):
        table[row : row + 1, :] = vector[...].astype(jnp.float32)
    by_gene[...] = table[...].T
    own = rows_of(person(where), 0)
    width = coef.shape[1]
    for block in range(width // LANES):
        cols = slice(block * LANES, (block + 1) * LANES)
        mask = block_mask(where, by_gene[...], block, width // 4)
        coef[:, cols] = (mask * coef_start[:, cols]).astype(jnp.bfloat16)
        mask = block_mask(where, by_gene[own, :], block, width // 4)
        coef_own[:, cols] = mask * coef_start[own, cols]


def update_kernel(total, first, where, by_gene, near, far, coef_own, base, *refs):
    own = rows_of(person(where), 0)
    table = by_gene[own, :]
    width = coef_own.shape[1]
    penalty, step = table[:, PENALTY : PENALTY + 1], table[:, STEP : STEP + 1]
    cut = step * penalty
    lane = lax.broadcasted_iota(jnp.int32, (OWN, LANES), 1)
    high = low = jnp.zeros((OWN, LANES), jnp.float32)
    for block in range(width // LANES):
        cols = slice(block * LANES, (block + 1) * LANES)
        mask = block_mask(where, table, block, width // 4)
        used = base[own, cols] if first else base[:, cols]
        grad = (near[:OWN, cols] + far[:, cols].astype(jnp.float32)) / total - used.astype(jnp.float32)
        moved = coef_own[:, cols] + step * grad
        size = jnp.maximum(jnp.abs(moved) - cut * l1_share, 0.0)
        kept = mask * jnp.where(moved < 0, -size, size) / (1.0 + cut * (1.0 - l1_share))
        if first:
            refs[0][:, cols] = kept
            peak = jnp.max(mask * jnp.abs(grad) / penalty, axis=1, keepdims=True)
            rounded = peak.astype(jnp.bfloat16).astype(jnp.float32)
            high = jnp.where(lane == block, rounded, high)
            low = jnp.where(lane == block + width // LANES, peak - rounded, low)
        refs[-1][:, cols] = kept.astype(jnp.bfloat16)
    if first:
        refs[-1][:, width:] = (high + low).astype(jnp.bfloat16)


def output_kernel(where, *refs):
    *pieces, out = refs

    def put(rows, piece):
        out[rows, :] = piece.astype(jnp.float32)

    place(person(where), pieces, put)


def in_vmem(array):
    return pltpu.with_memory_space_constraint(array, pltpu.VMEM)


def specs(count):
    vmem = pl.BlockSpec(memory_space=pltpu.VMEM)
    return [pl.BlockSpec(memory_space=pltpu.SMEM)] + [vmem] * count


def cut_columns(where, genotypes, reach):
    half = pltpu.VMEM((genotypes.shape[0], reach), genotypes.dtype)
    return pl.pallas_call(
        cut_kernel,
        out_shape=[half, half],
        in_specs=[pl.BlockSpec(memory_space=pltpu.SMEM), pl.BlockSpec(memory_space=pltpu.HBM)],
        out_specs=[pl.BlockSpec(memory_space=pltpu.VMEM)] * 2,
        scratch_shapes=[pltpu.SemaphoreType.DMA((2 * COPIES,))],
        compiler_params=pltpu.CompilerParams(vmem_limit_bytes=8 << 20),
    )(where, pltpu.with_memory_space_constraint(genotypes, pltpu.HBM))


def cost(people, blocks, products):
    flops = 2 * products * people * blocks.shape[0] * blocks.shape[1]
    return pl.CostEstimate(flops=flops, bytes_accessed=0, transcendentals=0)


def early_part(where, blocks, target, coef):
    operands = [in_vmem(v) for v in (*blocks, target, coef)]
    return pl.pallas_call(
        early_kernel,
        out_shape=pltpu.VMEM(target.shape, jnp.float32),
        in_specs=specs(len(operands)),
        out_specs=pl.BlockSpec(memory_space=pltpu.VMEM),
        compiler_params=pltpu.CompilerParams(vmem_limit_bytes=8 << 20),
        cost_estimate=pl.CostEstimate(flops=0, bytes_accessed=0, transcendentals=0),
    )(where, *operands)


def local_grad(where, blocks, target, pieces):
    people, genes = target.shape
    width = 4 * blocks[0].shape[1]
    operands = [in_vmem(v) for v in (*blocks, target, *pieces)]
    outs = [pltpu.VMEM((2 * OWN * len(NEAR), width), jnp.float32)]
    outs += [pltpu.VMEM((2 * OWN * len(hops), width), jnp.bfloat16) for hops in GIVE]
    scratch = [pltpu.VMEM((genes, width), jnp.float32), pltpu.VMEM((genes, people), jnp.bfloat16)]
    if len(pieces) > 1:
        outs.append(pltpu.VMEM((width // LANES, genes), jnp.float32))
        scratch.append(pltpu.VMEM((genes, width), jnp.bfloat16))
        scratch.append(pltpu.VMEM((genes, LANES), jnp.bfloat16))
    return pl.pallas_call(
        functools.partial(turn_kernel, len(pieces)),
        out_shape=outs,
        in_specs=specs(len(operands)),
        out_specs=[pl.BlockSpec(memory_space=pltpu.VMEM)] * len(outs),
        scratch_shapes=scratch,
        compiler_params=pltpu.CompilerParams(vmem_limit_bytes=20 << 20),
        cost_estimate=cost(people, jax.ShapeDtypeStruct((genes, width), jnp.bfloat16), 2),
    )(where, *operands)


def small_call(kernel, where, operands, outs, scratch=()):
    return pl.pallas_call(
        kernel,
        out_shape=[pltpu.VMEM(shape, dtype) for shape, dtype in outs],
        in_specs=specs(len(operands)),
        out_specs=[pl.BlockSpec(memory_space=pltpu.VMEM)] * len(outs),
        scratch_shapes=list(scratch),
        compiler_params=pltpu.CompilerParams(vmem_limit_bytes=8 << 20),
    )(where, *[in_vmem(v) for v in operands])


def swap(block, hop):
    count = lax.axis_size("people")
    return lax.ppermute(block, "people", [(i, i ^ hop) for i in range(count)])


def sum_to_owner(keep, gives):
    part, waiting = {}, []
    for hops, give in zip(GIVE, gives):
        give, *ready = lax.optimization_barrier((give, *[part[hop] for hop in waiting]))
        part.update(zip(waiting, ready))
        got = swap(give, SIDE)
        for n, hop in enumerate(hops):
            at = NEAR.index(hop) * 2 * OWN
            total = keep[at : at + 2 * OWN] + got[2 * n * OWN : 2 * (n + 1) * OWN]
            part[hop] = total.astype(jnp.bfloat16) if hop else total
        waiting = hops
    total = part[0]
    for hop in (6, 4, 2):
        total = total + swap(part[hop], hop)
    return total, swap(total[OWN:].astype(jnp.bfloat16), MIRROR)


def gather_rows(own):
    pair = jnp.concatenate([own, swap(own, MIRROR)], axis=0)
    got = {0: pair, 2: swap(pair, 2), 6: swap(pair, 6)}
    beside = swap(pair, SIDE)
    pair, *_ = lax.optimization_barrier((pair, got[6], beside))
    got[4] = swap(pair, 4)
    return [got[hop] for hop in NEAR] + [beside] + [swap(got[hop], SIDE) for hop in NEAR[1:]]


def on_device(
    genotypes, expression, coef_start, penalty, step_size, window_start, window_end, active_blocks
):
    v_local = genotypes.shape[1]
    total = genotypes.shape[0] * lax.axis_size("people")
    genes, width = coef_start.shape
    reach = (width - v_local) // 2
    count = lax.axis_size("genome")
    sibling = [(i, i ^ 1) for i in range(count)]
    beyond = [(i, i + 1 if i % 2 else i - 1) for i in range(count)]
    beyond = [(source, target) for source, target in beyond if 0 <= target < count]
    where = lax.axis_index(("genome", "people")).astype(jnp.int32)[None]
    vectors = [v[None] for v in (window_start, window_end, penalty, step_size)]
    by_gene, coef, coef_own = small_call(
        start_kernel,
        where,
        [active_blocks.T, *vectors, coef_start],
        [((genes, LANES), jnp.float32), ((genes, width), jnp.bfloat16), ((OWN, width), jnp.float32)],
        [pltpu.VMEM((LANES, genes), jnp.float32)],
    )

    away, beside = cut_columns(where, genotypes, reach)
    slow = lax.ppermute(away, "genome", beyond)
    fast = lax.ppermute(beside, "genome", sibling)
    blocks = [slow, away, beside, fast]
    part = early_part(where, blocks[1:], expression, coef)
    keep, *gives = local_grad(where, blocks, part, [coef])
    near, far = sum_to_owner(keep, gives)
    coef_own, sent = small_call(
        functools.partial(update_kernel, total, True),
        where,
        [by_gene, near, far, coef_own, coef],
        [((OWN, width), jnp.float32), ((OWN, width + LANES), jnp.bfloat16)],
    )
    pieces = gather_rows(sent)

    keep, *gives, peaks = local_grad(where, blocks, expression, pieces)
    near, far = sum_to_owner(keep, gives)
    (last,) = small_call(
        functools.partial(update_kernel, total, False),
        where,
        [by_gene, near, far, coef_own, sent],
        [((OWN, width), jnp.bfloat16)],
    )
    pieces = gather_rows(last)
    coef = pl.pallas_call(
        output_kernel,
        out_shape=jax.ShapeDtypeStruct((genes, width), jnp.float32),
        in_specs=specs(len(pieces)),
        out_specs=pl.BlockSpec(memory_space=pltpu.VMEM),
        compiler_params=pltpu.CompilerParams(vmem_limit_bytes=8 << 20),
    )(where, *[in_vmem(piece) for piece in pieces])
    return (coef, peaks.T)


def solution(mesh):
    return jax.shard_map(
        on_device,
        mesh=mesh,
        in_specs=(
            P("people", "genome"),
            P("people", "genome"),
            P("genome", None),
            P("genome"),
            P("genome"),
            P("genome"),
            P("genome"),
            P("genome", None),
        ),
        out_specs=(P("genome", None), P("genome", None)),
        check_vma=False,
    )
```

```python
import functools

import jax
import jax.numpy as jnp
from jax import lax
from jax.experimental import pallas as pl
from jax.experimental.pallas import tpu as pltpu
from jax.sharding import PartitionSpec as P

l1_share = 0.5
SIDE, MIRROR = 1, 14
NEAR = (0, 2, 4, 6)
GIVE = ((6,), (4, 2), (0,))
OWN = 16
PEOPLE = 16
LANES = 128
START, END, PENALTY, STEP = 16, 17, 18, 19

TILE = 768
COPIES = 4
CUT = 256


def dot(a, b):
    return jnp.dot(a, b, preferred_element_type=jnp.float32)


def rows_of(me, hop):
    return pl.ds(pl.multiple_of((me ^ hop) * OWN, OWN), OWN)


def dot_t(a, b):
    return lax.dot_general(a, b, (((1,), (1,)), ((), ())), preferred_element_type=jnp.float32)


def person(where):
    return where[0] % PEOPLE


def place(me, pieces, put):
    for k, piece in enumerate(pieces):
        hop = NEAR[k % len(NEAR)] ^ (k // len(NEAR) * SIDE)
        put(rows_of(me, hop), piece[:OWN, :])
        put(rows_of(me, hop ^ MIRROR), piece[OWN:, :])


def cut_kernel(where, whole, away, beside, sems):
    people, reach = away.shape
    count = people // COPIES
    core = where[0] // PEOPLE % 2
    copies = []
    for n, (out, half) in enumerate(((away, core), (beside, 1 - core))):
        cols = pl.ds(pl.multiple_of(half * reach, reach), reach)
        for k in range(COPIES):
            rows = pl.ds(k * count, count)
            sem = sems.at[n * COPIES + k]
            copies.append(pltpu.make_async_copy(whole.at[rows, cols], out.at[rows, :], sem))
    for copy in copies:
        copy.start()
    for copy in copies:
        copy.wait()


def column_of(where, block, reach):
    core = where[0] // PEOPLE % 2
    return pl.multiple_of((block + core * (3 - 2 * block)) * reach, reach)


def fit(where, rows, blocks, coef):
    fitted = 0.0
    for i, block in blocks.items():
        reach = block.shape[1]
        fitted += dot_t(block[rows, :], coef[:, pl.ds(column_of(where, i, reach), reach)])
    return fitted


def early_kernel(where, second, third, fourth, target, coef, part):
    blocks = {1: second, 2: third, 3: fourth}
    for step in range(0, target.shape[0], TILE):
        rows = pl.ds(step, TILE)
        part[rows, :] = target[rows, :].astype(jnp.float32) - fit(where, rows, blocks, coef)


def turn_kernel(n_pieces, *refs):
    where, *refs = refs
    blocks, refs = refs[:4], refs[4:]
    target, *refs = refs
    pieces, refs = refs[:n_pieces], refs[n_pieces:]
    keep, *refs = refs
    gives, refs = refs[: len(GIVE)], refs[len(GIVE) :]
    reach = blocks[0].shape[1]
    width = 4 * reach
    me = person(where)
    if n_pieces > 1:
        peaks, grad, resid_t, coef, tail = refs

        def put(rows, piece):
            coef[rows, :] = piece[:, :width]
            tail[rows, :] = piece[:, width:]

        place(me, pieces, put)
        count = peaks.shape[0]
        flat = tail[...].astype(jnp.float32).T
        peaks[...] = flat[:count, :] + flat[count : 2 * count, :]
    else:
        (coef,) = pieces
        grad, resid_t = refs

    last = {0: blocks[0]} if n_pieces == 1 else dict(enumerate(blocks))
    for step in range(0, target.shape[0], TILE):
        rows = pl.ds(step, TILE)
        resid = target[rows, :].astype(jnp.float32) - fit(where, rows, last, coef)
        resid_t[:, rows] = resid.astype(jnp.bfloat16).T

    for i, block in enumerate(blocks):
        for j in range(0, reach, CUT):
            cols = pl.ds(pl.multiple_of(column_of(where, i, reach) + j, CUT), CUT)
            grad[:, cols] = dot(resid_t[...], block[:, j : j + CUT])

    def read(hop):
        rows = rows_of(me, hop)
        return grad[rows, :] + coef[rows, :].astype(jnp.float32) * target.shape[0]

    for give, hops in zip(gives, GIVE):
        for n, hop in enumerate(hops):
            for k, far in enumerate((0, MIRROR)):
                at = (2 * n + k) * OWN
                give[at : at + OWN, :] = read(hop ^ SIDE ^ far).astype(jnp.bfloat16)
    for n, hop in enumerate(NEAR):
        for k, far in enumerate((0, MIRROR)):
            at = (2 * n + k) * OWN
            keep[at : at + OWN, :] = read(hop ^ far)


def block_mask(where, table, block, reach):
    rows = table.shape[0]
    first = where[0] // PEOPLE * (2 * reach) - reach + block * LANES
    column = lax.broadcasted_iota(jnp.int32, (rows, LANES), 1) + first
    column = column.astype(jnp.float32)
    inside = (column >= table[:, START : START + 1]) & (column < table[:, END : END + 1])
    return jnp.where(inside & (table[:, block : block + 1] > 0), 1.0, 0.0)


def start_kernel(where, active, *refs):
    *vectors, coef_start, by_gene, coef, coef_own, table = refs
    table[...] = jnp.zeros(table.shape, jnp.float32)
    table[: active.shape[0], :] = active[...].astype(jnp.float32)
    for row, vector in zip((START, END, PENALTY, STEP), vectors):
        table[row : row + 1, :] = vector[...].astype(jnp.float32)
    by_gene[...] = table[...].T
    own = rows_of(person(where), 0)
    width = coef.shape[1]
    for block in range(width // LANES):
        cols = slice(block * LANES, (block + 1) * LANES)
        mask = block_mask(where, by_gene[...], block, width // 4)
        coef[:, cols] = (mask * coef_start[:, cols]).astype(jnp.bfloat16)
        mask = block_mask(where, by_gene[own, :], block, width // 4)
        coef_own[:, cols] = mask * coef_start[own, cols]


def update_kernel(total, first, where, by_gene, near, far, coef_own, base, *refs):
    own = rows_of(person(where), 0)
    table = by_gene[own, :]
    width = coef_own.shape[1]
    penalty, step = table[:, PENALTY : PENALTY + 1], table[:, STEP : STEP + 1]
    cut = step * penalty
    lane = lax.broadcasted_iota(jnp.int32, (OWN, LANES), 1)
    high = low = jnp.zeros((OWN, LANES), jnp.float32)
    for block in range(width // LANES):
        cols = slice(block * LANES, (block + 1) * LANES)
        mask = block_mask(where, table, block, width // 4)
        used = base[own, cols] if first else base[:, cols]
        grad = (near[:OWN, cols] + far[:, cols].astype(jnp.float32)) / total - used.astype(jnp.float32)
        moved = coef_own[:, cols] + step * grad
        size = jnp.maximum(jnp.abs(moved) - cut * l1_share, 0.0)
        kept = mask * jnp.where(moved < 0, -size, size) / (1.0 + cut * (1.0 - l1_share))
        if first:
            refs[0][:, cols] = kept
            peak = jnp.max(mask * jnp.abs(grad) / penalty, axis=1, keepdims=True)
            rounded = peak.astype(jnp.bfloat16).astype(jnp.float32)
            high = jnp.where(lane == block, rounded, high)
            low = jnp.where(lane == block + width // LANES, peak - rounded, low)
        refs[-1][:, cols] = kept.astype(jnp.bfloat16)
    if first:
        refs[-1][:, width:] = (high + low).astype(jnp.bfloat16)


def output_kernel(where, *refs):
    *pieces, out = refs

    def put(rows, piece):
        out[rows, :] = piece.astype(jnp.float32)

    place(person(where), pieces, put)


def in_vmem(array):
    return pltpu.with_memory_space_constraint(array, pltpu.VMEM)


def specs(count):
    vmem = pl.BlockSpec(memory_space=pltpu.VMEM)
    return [pl.BlockSpec(memory_space=pltpu.SMEM)] + [vmem] * count


def cut_columns(where, genotypes, reach):
    half = pltpu.VMEM((genotypes.shape[0], reach), genotypes.dtype)
    return pl.pallas_call(
        cut_kernel,
        out_shape=[half, half],
        in_specs=[pl.BlockSpec(memory_space=pltpu.SMEM), pl.BlockSpec(memory_space=pltpu.HBM)],
        out_specs=[pl.BlockSpec(memory_space=pltpu.VMEM)] * 2,
        scratch_shapes=[pltpu.SemaphoreType.DMA((2 * COPIES,))],
        compiler_params=pltpu.CompilerParams(vmem_limit_bytes=8 << 20),
    )(where, pltpu.with_memory_space_constraint(genotypes, pltpu.HBM))


def cost(people, blocks, products):
    flops = 2 * products * people * blocks.shape[0] * blocks.shape[1]
    return pl.CostEstimate(flops=flops, bytes_accessed=0, transcendentals=0)


def early_part(where, blocks, target, coef):
    operands = [in_vmem(v) for v in (*blocks, target, coef)]
    return pl.pallas_call(
        early_kernel,
        out_shape=pltpu.VMEM(target.shape, jnp.float32),
        in_specs=specs(len(operands)),
        out_specs=pl.BlockSpec(memory_space=pltpu.VMEM),
        compiler_params=pltpu.CompilerParams(vmem_limit_bytes=8 << 20),
        cost_estimate=pl.CostEstimate(flops=0, bytes_accessed=0, transcendentals=0),
    )(where, *operands)


def local_grad(where, blocks, target, pieces):
    people, genes = target.shape
    width = 4 * blocks[0].shape[1]
    operands = [in_vmem(v) for v in (*blocks, target, *pieces)]
    outs = [pltpu.VMEM((2 * OWN * len(NEAR), width), jnp.float32)]
    outs += [pltpu.VMEM((2 * OWN * len(hops), width), jnp.bfloat16) for hops in GIVE]
    scratch = [pltpu.VMEM((genes, width), jnp.float32), pltpu.VMEM((genes, people), jnp.bfloat16)]
    if len(pieces) > 1:
        outs.append(pltpu.VMEM((width // LANES, genes), jnp.float32))
        scratch.append(pltpu.VMEM((genes, width), jnp.bfloat16))
        scratch.append(pltpu.VMEM((genes, LANES), jnp.bfloat16))
    return pl.pallas_call(
        functools.partial(turn_kernel, len(pieces)),
        out_shape=outs,
        in_specs=specs(len(operands)),
        out_specs=[pl.BlockSpec(memory_space=pltpu.VMEM)] * len(outs),
        scratch_shapes=scratch,
        compiler_params=pltpu.CompilerParams(vmem_limit_bytes=20 << 20),
        cost_estimate=cost(people, jax.ShapeDtypeStruct((genes, width), jnp.bfloat16), 2),
    )(where, *operands)


def small_call(kernel, where, operands, outs, scratch=()):
    return pl.pallas_call(
        kernel,
        out_shape=[pltpu.VMEM(shape, dtype) for shape, dtype in outs],
        in_specs=specs(len(operands)),
        out_specs=[pl.BlockSpec(memory_space=pltpu.VMEM)] * len(outs),
        scratch_shapes=list(scratch),
        compiler_params=pltpu.CompilerParams(vmem_limit_bytes=8 << 20),
    )(where, *[in_vmem(v) for v in operands])


def swap(block, hop):
    count = lax.axis_size("people")
    return lax.ppermute(block, "people", [(i, i ^ hop) for i in range(count)])


def sum_to_owner(keep, gives):
    part = {}
    for hops, give in zip(GIVE, gives):
        got = swap(give, SIDE)
        for n, hop in enumerate(hops):
            at = NEAR.index(hop) * 2 * OWN
            part[hop] = keep[at : at + 2 * OWN] + got[2 * n * OWN : 2 * (n + 1) * OWN]
    total = part[0]
    for hop in (6, 4, 2):
        total = total + swap(part[hop].astype(jnp.bfloat16), hop)
    return total, swap(total[OWN:].astype(jnp.bfloat16), MIRROR)


def gather_rows(own):
    pair = jnp.concatenate([own, swap(own, MIRROR)], axis=0)
    got = {0: pair, 2: swap(pair, 2), 6: swap(pair, 6)}
    beside = swap(pair, SIDE)
    pair, *_ = lax.optimization_barrier((pair, got[6], beside))
    got[4] = swap(pair, 4)
    return [got[hop] for hop in NEAR] + [beside] + [swap(got[hop], SIDE) for hop in NEAR[1:]]


def on_device(
    genotypes, expression, coef_start, penalty, step_size, window_start, window_end, active_blocks
):
    v_local = genotypes.shape[1]
    total = genotypes.shape[0] * lax.axis_size("people")
    genes, width = coef_start.shape
    reach = (width - v_local) // 2
    count = lax.axis_size("genome")
    sibling = [(i, i ^ 1) for i in range(count)]
    beyond = [(i, i + 1 if i % 2 else i - 1) for i in range(count)]
    beyond = [(source, target) for source, target in beyond if 0 <= target < count]
    where = lax.axis_index(("genome", "people")).astype(jnp.int32)[None]
    vectors = [v[None] for v in (window_start, window_end, penalty, step_size)]
    by_gene, coef, coef_own = small_call(
        start_kernel,
        where,
        [active_blocks.T, *vectors, coef_start],
        [((genes, LANES), jnp.float32), ((genes, width), jnp.bfloat16), ((OWN, width), jnp.float32)],
        [pltpu.VMEM((LANES, genes), jnp.float32)],
    )

    away, beside = cut_columns(where, genotypes, reach)
    slow = lax.ppermute(away, "genome", beyond)
    fast = lax.ppermute(beside, "genome", sibling)
    blocks = [slow, away, beside, fast]
    part = early_part(where, blocks[1:], expression, coef)
    keep, *gives = local_grad(where, blocks, part, [coef])
    near, far = sum_to_owner(keep, gives)
    coef_own, sent = small_call(
        functools.partial(update_kernel, total, True),
        where,
        [by_gene, near, far, coef_own, coef],
        [((OWN, width), jnp.float32), ((OWN, width + LANES), jnp.bfloat16)],
    )
    pieces = gather_rows(sent)

    keep, *gives, peaks = local_grad(where, blocks, expression, pieces)
    near, far = sum_to_owner(keep, gives)
    (last,) = small_call(
        functools.partial(update_kernel, total, False),
        where,
        [by_gene, near, far, coef_own, sent],
        [((OWN, width), jnp.bfloat16)],
    )
    pieces = gather_rows(last)
    coef = pl.pallas_call(
        output_kernel,
        out_shape=jax.ShapeDtypeStruct((genes, width), jnp.float32),
        in_specs=specs(len(pieces)),
        out_specs=pl.BlockSpec(memory_space=pltpu.VMEM),
        compiler_params=pltpu.CompilerParams(vmem_limit_bytes=8 << 20),
    )(where, *[in_vmem(piece) for piece in pieces])
    return (coef, peaks.T)


def solution(mesh):
    return jax.shard_map(
        on_device,
        mesh=mesh,
        in_specs=(
            P("people", "genome"),
            P("people", "genome"),
            P("genome", None),
            P("genome"),
            P("genome"),
            P("genome"),
            P("genome"),
            P("genome", None),
        ),
        out_specs=(P("genome", None), P("genome", None)),
        check_vma=False,
    )
```

```python
import functools

import jax
import jax.numpy as jnp
from jax import lax
from jax.experimental import pallas as pl
from jax.experimental.pallas import tpu as pltpu
from jax.sharding import PartitionSpec as P

l1_share = 0.5
SIDE, MIRROR = 1, 14
NEAR = (0, 2, 4, 6)
GIVE = ((6,), (4, 2), (0,))
OWN = 16
PEOPLE = 16
LANES = 128
START, END, PENALTY, STEP = 16, 17, 18, 19

TILE = 768
COPIES = 4
CUT = 256


def dot(a, b):
    return jnp.dot(a, b, preferred_element_type=jnp.float32)


def rows_of(me, hop):
    return pl.ds(pl.multiple_of((me ^ hop) * OWN, OWN), OWN)


def dot_t(a, b):
    return lax.dot_general(a, b, (((1,), (1,)), ((), ())), preferred_element_type=jnp.float32)


def person(where):
    return where[0] % PEOPLE


def place(me, pieces, put):
    for k, piece in enumerate(pieces):
        hop = NEAR[k % len(NEAR)] ^ (k // len(NEAR) * SIDE)
        put(rows_of(me, hop), piece[:OWN, :])
        put(rows_of(me, hop ^ MIRROR), piece[OWN:, :])


def cut_kernel(where, whole, away, beside, sems):
    people, reach = away.shape
    count = people // COPIES
    core = where[0] // PEOPLE % 2
    copies = []
    for n, (out, half) in enumerate(((away, core), (beside, 1 - core))):
        cols = pl.ds(pl.multiple_of(half * reach, reach), reach)
        for k in range(COPIES):
            rows = pl.ds(k * count, count)
            sem = sems.at[n * COPIES + k]
            copies.append(pltpu.make_async_copy(whole.at[rows, cols], out.at[rows, :], sem))
    for copy in copies:
        copy.start()
    for copy in copies:
        copy.wait()


def column_of(where, block, reach):
    core = where[0] // PEOPLE % 2
    return pl.multiple_of((block + core * (3 - 2 * block)) * reach, reach)


def fit(where, rows, blocks, coef):
    fitted = 0.0
    for i, block in blocks.items():
        reach = block.shape[1]
        fitted += dot_t(block[rows, :], coef[:, pl.ds(column_of(where, i, reach), reach)])
    return fitted


def early_kernel(where, second, third, fourth, target, coef, part):
    blocks = {1: second, 2: third, 3: fourth}
    for step in range(0, target.shape[0], TILE):
        rows = pl.ds(step, TILE)
        part[rows, :] = target[rows, :].astype(jnp.float32) - fit(where, rows, blocks, coef)


def turn_kernel(n_pieces, *refs):
    where, *refs = refs
    blocks, refs = refs[:4], refs[4:]
    target, *refs = refs
    pieces, refs = refs[:n_pieces], refs[n_pieces:]
    keep, *refs = refs
    gives, refs = refs[: len(GIVE)], refs[len(GIVE) :]
    reach = blocks[0].shape[1]
    width = 4 * reach
    me = person(where)
    if n_pieces > 1:
        peaks, grad, resid_t, coef, tail = refs

        def put(rows, piece):
            coef[rows, :] = piece[:, :width]
            tail[rows, :] = piece[:, width:]

        place(me, pieces, put)
        count = peaks.shape[0]
        flat = tail[...].astype(jnp.float32).T
        peaks[...] = flat[:count, :] + flat[count : 2 * count, :]
    else:
        (coef,) = pieces
        grad, resid_t = refs

    last = {0: blocks[0]} if n_pieces == 1 else dict(enumerate(blocks))
    for step in range(0, target.shape[0], TILE):
        rows = pl.ds(step, TILE)
        resid = target[rows, :].astype(jnp.float32) - fit(where, rows, last, coef)
        resid_t[:, rows] = resid.astype(jnp.bfloat16).T

    for i, block in enumerate(blocks):
        for j in range(0, reach, CUT):
            cols = pl.ds(pl.multiple_of(column_of(where, i, reach) + j, CUT), CUT)
            grad[:, cols] = dot(resid_t[...], block[:, j : j + CUT])

    def read(hop):
        rows = rows_of(me, hop)
        return grad[rows, :] + coef[rows, :].astype(jnp.float32) * target.shape[0]

    for give, hops in zip(gives, GIVE):
        for n, hop in enumerate(hops):
            for k, far in enumerate((0, MIRROR)):
                at = (2 * n + k) * OWN
                give[at : at + OWN, :] = read(hop ^ SIDE ^ far).astype(jnp.bfloat16)
    for n, hop in enumerate(NEAR):
        for k, far in enumerate((0, MIRROR)):
            at = (2 * n + k) * OWN
            keep[at : at + OWN, :] = read(hop ^ far)


def block_mask(where, table, block, reach):
    rows = table.shape[0]
    first = where[0] // PEOPLE * (2 * reach) - reach + block * LANES
    column = lax.broadcasted_iota(jnp.int32, (rows, LANES), 1) + first
    column = column.astype(jnp.float32)
    inside = (column >= table[:, START : START + 1]) & (column < table[:, END : END + 1])
    return jnp.where(inside & (table[:, block : block + 1] > 0), 1.0, 0.0)


def start_kernel(where, active, *refs):
    *vectors, coef_start, by_gene, coef, coef_own, table = refs
    table[...] = jnp.zeros(table.shape, jnp.float32)
    table[: active.shape[0], :] = active[...].astype(jnp.float32)
    for row, vector in zip((START, END, PENALTY, STEP), vectors):
        table[row : row + 1, :] = vector[...].astype(jnp.float32)
    by_gene[...] = table[...].T
    low, high = slice(0, OWN), slice(OWN, 2 * OWN)
    width = coef.shape[1]
    for block in range(width // LANES):
        cols = slice(block * LANES, (block + 1) * LANES)
        mask = block_mask(where, by_gene[...], block, width // 4)
        coef[:, cols] = (mask * coef_start[:, cols]).astype(jnp.bfloat16)
        for part, hop in ((low, 0), (high, MIRROR)):
            rows = rows_of(person(where), hop)
            mask = block_mask(where, by_gene[rows, :], block, width // 4)
            coef_own[part, cols] = mask * coef_start[rows, cols]


def update_kernel(total, first, where, by_gene, near, far, coef_own, base, *refs):
    width = coef_own.shape[1]
    lane = lax.broadcasted_iota(jnp.int32, (OWN, LANES), 1)
    for half, hop in enumerate((0, MIRROR)):
        rows = rows_of(person(where), hop)
        part, other = slice(half * OWN, (half + 1) * OWN), slice((1 - half) * OWN, (2 - half) * OWN)
        table = by_gene[rows, :]
        penalty, step = table[:, PENALTY : PENALTY + 1], table[:, STEP : STEP + 1]
        cut = step * penalty
        high = low = jnp.zeros((OWN, LANES), jnp.float32)
        for block in range(width // LANES):
            cols = slice(block * LANES, (block + 1) * LANES)
            mask = block_mask(where, table, block, width // 4)
            used = base[rows, cols] if first else base[part, cols]
            sums = near[part, cols].astype(jnp.float32) + far[other, cols].astype(jnp.float32)
            grad = sums / total - used.astype(jnp.float32)
            moved = coef_own[part, cols] + step * grad
            size = jnp.maximum(jnp.abs(moved) - cut * l1_share, 0.0)
            kept = mask * jnp.where(moved < 0, -size, size) / (1.0 + cut * (1.0 - l1_share))
            if first:
                refs[0][part, cols] = kept
                peak = jnp.max(mask * jnp.abs(grad) / penalty, axis=1, keepdims=True)
                rounded = peak.astype(jnp.bfloat16).astype(jnp.float32)
                high = jnp.where(lane == block, rounded, high)
                low = jnp.where(lane == block + width // LANES, peak - rounded, low)
            refs[-1][part, cols] = kept.astype(jnp.bfloat16)
        if first:
            refs[-1][part, width:] = (high + low).astype(jnp.bfloat16)


def output_kernel(where, *refs):
    *pieces, out = refs

    def put(rows, piece):
        out[rows, :] = piece.astype(jnp.float32)

    place(person(where), pieces, put)


def in_vmem(array):
    return pltpu.with_memory_space_constraint(array, pltpu.VMEM)


def specs(count):
    vmem = pl.BlockSpec(memory_space=pltpu.VMEM)
    return [pl.BlockSpec(memory_space=pltpu.SMEM)] + [vmem] * count


def cut_columns(where, genotypes, reach):
    half = pltpu.VMEM((genotypes.shape[0], reach), genotypes.dtype)
    return pl.pallas_call(
        cut_kernel,
        out_shape=[half, half],
        in_specs=[pl.BlockSpec(memory_space=pltpu.SMEM), pl.BlockSpec(memory_space=pltpu.HBM)],
        out_specs=[pl.BlockSpec(memory_space=pltpu.VMEM)] * 2,
        scratch_shapes=[pltpu.SemaphoreType.DMA((2 * COPIES,))],
        compiler_params=pltpu.CompilerParams(vmem_limit_bytes=8 << 20),
    )(where, pltpu.with_memory_space_constraint(genotypes, pltpu.HBM))


def cost(people, blocks, products):
    flops = 2 * products * people * blocks.shape[0] * blocks.shape[1]
    return pl.CostEstimate(flops=flops, bytes_accessed=0, transcendentals=0)


def early_part(where, blocks, target, coef):
    operands = [in_vmem(v) for v in (*blocks, target, coef)]
    return pl.pallas_call(
        early_kernel,
        out_shape=pltpu.VMEM(target.shape, jnp.float32),
        in_specs=specs(len(operands)),
        out_specs=pl.BlockSpec(memory_space=pltpu.VMEM),
        compiler_params=pltpu.CompilerParams(vmem_limit_bytes=8 << 20),
        cost_estimate=pl.CostEstimate(flops=0, bytes_accessed=0, transcendentals=0),
    )(where, *operands)


def local_grad(where, blocks, target, pieces):
    people, genes = target.shape
    width = 4 * blocks[0].shape[1]
    operands = [in_vmem(v) for v in (*blocks, target, *pieces)]
    outs = [pltpu.VMEM((2 * OWN * len(NEAR), width), jnp.float32)]
    outs += [pltpu.VMEM((2 * OWN * len(hops), width), jnp.bfloat16) for hops in GIVE]
    scratch = [pltpu.VMEM((genes, width), jnp.float32), pltpu.VMEM((genes, people), jnp.bfloat16)]
    if len(pieces) > 1:
        outs.append(pltpu.VMEM((width // LANES, genes), jnp.float32))
        scratch.append(pltpu.VMEM((genes, width), jnp.bfloat16))
        scratch.append(pltpu.VMEM((genes, LANES), jnp.bfloat16))
    return pl.pallas_call(
        functools.partial(turn_kernel, len(pieces)),
        out_shape=outs,
        in_specs=specs(len(operands)),
        out_specs=[pl.BlockSpec(memory_space=pltpu.VMEM)] * len(outs),
        scratch_shapes=scratch,
        compiler_params=pltpu.CompilerParams(vmem_limit_bytes=20 << 20),
        cost_estimate=cost(people, jax.ShapeDtypeStruct((genes, width), jnp.bfloat16), 2),
    )(where, *operands)


def small_call(kernel, where, operands, outs, scratch=()):
    return pl.pallas_call(
        kernel,
        out_shape=[pltpu.VMEM(shape, dtype) for shape, dtype in outs],
        in_specs=specs(len(operands)),
        out_specs=[pl.BlockSpec(memory_space=pltpu.VMEM)] * len(outs),
        scratch_shapes=list(scratch),
        compiler_params=pltpu.CompilerParams(vmem_limit_bytes=8 << 20),
    )(where, *[in_vmem(v) for v in operands])


def swap(block, hop):
    count = lax.axis_size("people")
    return lax.ppermute(block, "people", [(i, i ^ hop) for i in range(count)])


def sum_to_owner(keep, gives):
    part = {}
    for hops, give in zip(GIVE, gives):
        got = swap(give, SIDE)
        for n, hop in enumerate(hops):
            at = NEAR.index(hop) * 2 * OWN
            part[hop] = keep[at : at + 2 * OWN] + got[2 * n * OWN : 2 * (n + 1) * OWN]
    total = part[0]
    for hop in (6, 4, 2):
        total = total + swap(part[hop].astype(jnp.bfloat16), hop)
    near = total.astype(jnp.bfloat16)
    return near, swap(near, MIRROR)


def gather_rows(pair):
    got = {0: pair, 2: swap(pair, 2), 6: swap(pair, 6)}
    beside = swap(pair, SIDE)
    pair, *_ = lax.optimization_barrier((pair, got[6], beside))
    got[4] = swap(pair, 4)
    return [got[hop] for hop in NEAR] + [beside] + [swap(got[hop], SIDE) for hop in NEAR[1:]]


def on_device(
    genotypes, expression, coef_start, penalty, step_size, window_start, window_end, active_blocks
):
    v_local = genotypes.shape[1]
    total = genotypes.shape[0] * lax.axis_size("people")
    genes, width = coef_start.shape
    reach = (width - v_local) // 2
    count = lax.axis_size("genome")
    sibling = [(i, i ^ 1) for i in range(count)]
    beyond = [(i, i + 1 if i % 2 else i - 1) for i in range(count)]
    beyond = [(source, target) for source, target in beyond if 0 <= target < count]
    where = lax.axis_index(("genome", "people")).astype(jnp.int32)[None]
    vectors = [v[None] for v in (window_start, window_end, penalty, step_size)]
    by_gene, coef, coef_own = small_call(
        start_kernel,
        where,
        [active_blocks.T, *vectors, coef_start],
        [((genes, LANES), jnp.float32), ((genes, width), jnp.bfloat16), ((2 * OWN, width), jnp.float32)],
        [pltpu.VMEM((LANES, genes), jnp.float32)],
    )

    away, beside = cut_columns(where, genotypes, reach)
    slow = lax.ppermute(away, "genome", beyond)
    fast = lax.ppermute(beside, "genome", sibling)
    blocks = [slow, away, beside, fast]
    part = early_part(where, blocks[1:], expression, coef)
    keep, *gives = local_grad(where, blocks, part, [coef])
    near, far = sum_to_owner(keep, gives)
    coef_own, sent = small_call(
        functools.partial(update_kernel, total, True),
        where,
        [by_gene, near, far, coef_own, coef],
        [((2 * OWN, width), jnp.float32), ((2 * OWN, width + LANES), jnp.bfloat16)],
    )
    pieces = gather_rows(sent)

    keep, *gives, peaks = local_grad(where, blocks, expression, pieces)
    near, far = sum_to_owner(keep, gives)
    (last,) = small_call(
        functools.partial(update_kernel, total, False),
        where,
        [by_gene, near, far, coef_own, sent],
        [((2 * OWN, width), jnp.bfloat16)],
    )
    pieces = gather_rows(last)
    coef = pl.pallas_call(
        output_kernel,
        out_shape=jax.ShapeDtypeStruct((genes, width), jnp.float32),
        in_specs=specs(len(pieces)),
        out_specs=pl.BlockSpec(memory_space=pltpu.VMEM),
        compiler_params=pltpu.CompilerParams(vmem_limit_bytes=8 << 20),
    )(where, *[in_vmem(piece) for piece in pieces])
    return (coef, peaks.T)


def solution(mesh):
    return jax.shard_map(
        on_device,
        mesh=mesh,
        in_specs=(
            P("people", "genome"),
            P("people", "genome"),
            P("genome", None),
            P("genome"),
            P("genome"),
            P("genome"),
            P("genome"),
            P("genome", None),
        ),
        out_specs=(P("genome", None), P("genome", None)),
        check_vma=False,
    )
```

```python
import functools

import jax
import jax.numpy as jnp
from jax import lax
from jax.experimental import pallas as pl
from jax.experimental.pallas import tpu as pltpu
from jax.sharding import PartitionSpec as P

l1_share = 0.5
SIDE, MIRROR = 1, 14
NEAR = (0, 2, 4, 6)
GIVE = ((6,), (4, 2), (0,))
OWN = 16
PEOPLE = 16
LANES = 128
START, END, PENALTY, STEP = 16, 17, 18, 19

TILE = 768
COPIES = 4
CUT = 256


def dot(a, b):
    return jnp.dot(a, b, preferred_element_type=jnp.float32)


def rows_of(me, hop):
    return pl.ds(pl.multiple_of((me ^ hop) * OWN, OWN), OWN)


def dot_t(a, b):
    return lax.dot_general(a, b, (((1,), (1,)), ((), ())), preferred_element_type=jnp.float32)


def person(where):
    return where[0] % PEOPLE


def place(me, pieces, put):
    for k, piece in enumerate(pieces):
        hop = NEAR[k % len(NEAR)] ^ (k // len(NEAR) * SIDE)
        put(rows_of(me, hop), piece[:OWN, :])
        put(rows_of(me, hop ^ MIRROR), piece[OWN:, :])


def cut_kernel(where, whole, away, beside, sems):
    people, reach = away.shape
    count = people // COPIES
    core = where[0] // PEOPLE % 2
    copies = []
    for n, (out, half) in enumerate(((away, core), (beside, 1 - core))):
        cols = pl.ds(pl.multiple_of(half * reach, reach), reach)
        for k in range(COPIES):
            rows = pl.ds(k * count, count)
            sem = sems.at[n * COPIES + k]
            copies.append(pltpu.make_async_copy(whole.at[rows, cols], out.at[rows, :], sem))
    for copy in copies:
        copy.start()
    for copy in copies:
        copy.wait()


def column_of(where, block, reach):
    core = where[0] // PEOPLE % 2
    return pl.multiple_of((block + core * (3 - 2 * block)) * reach, reach)


def fit(where, rows, blocks, coef):
    fitted = 0.0
    for i, block in blocks.items():
        reach = block.shape[1]
        fitted += dot_t(block[rows, :], coef[:, pl.ds(column_of(where, i, reach), reach)])
    return fitted


def early_kernel(where, second, third, fourth, target, coef, part):
    blocks = {1: second, 2: third, 3: fourth}
    for step in range(0, target.shape[0], TILE):
        rows = pl.ds(step, TILE)
        part[rows, :] = target[rows, :].astype(jnp.float32) - fit(where, rows, blocks, coef)


def turn_kernel(n_pieces, *refs):
    where, *refs = refs
    blocks, refs = refs[:4], refs[4:]
    target, *refs = refs
    pieces, refs = refs[:n_pieces], refs[n_pieces:]
    keep, *refs = refs
    gives, refs = refs[: len(GIVE)], refs[len(GIVE) :]
    reach = blocks[0].shape[1]
    width = 4 * reach
    me = person(where)
    if n_pieces > 1:
        grad, resid_t, coef = refs

        def put(rows, piece):
            coef[rows, :] = piece[...]

        place(me, pieces, put)
    else:
        (coef,) = pieces
        grad, resid_t = refs

    last = {0: blocks[0]} if n_pieces == 1 else dict(enumerate(blocks))
    for step in range(0, target.shape[0], TILE):
        rows = pl.ds(step, TILE)
        resid = target[rows, :].astype(jnp.float32) - fit(where, rows, last, coef)
        resid_t[:, rows] = resid.astype(jnp.bfloat16).T

    for i, block in enumerate(blocks):
        for j in range(0, reach, CUT):
            cols = pl.ds(pl.multiple_of(column_of(where, i, reach) + j, CUT), CUT)
            grad[:, cols] = dot(resid_t[...], block[:, j : j + CUT])

    def read(hop):
        rows = rows_of(me, hop)
        return grad[rows, :] + coef[rows, :].astype(jnp.float32) * target.shape[0]

    for give, hops in zip(gives, GIVE):
        for n, hop in enumerate(hops):
            for k, far in enumerate((0, MIRROR)):
                at = (2 * n + k) * OWN
                give[at : at + OWN, :] = read(hop ^ SIDE ^ far).astype(jnp.bfloat16)
    for n, hop in enumerate(NEAR):
        for k, far in enumerate((0, MIRROR)):
            at = (2 * n + k) * OWN
            keep[at : at + OWN, :] = read(hop ^ far)


def block_mask(where, table, block, reach):
    rows = table.shape[0]
    first = where[0] // PEOPLE * (2 * reach) - reach + block * LANES
    column = lax.broadcasted_iota(jnp.int32, (rows, LANES), 1) + first
    column = column.astype(jnp.float32)
    inside = (column >= table[:, START : START + 1]) & (column < table[:, END : END + 1])
    return jnp.where(inside & (table[:, block : block + 1] > 0), 1.0, 0.0)


def start_kernel(where, active, *refs):
    *vectors, coef_start, by_gene, coef, coef_own, table = refs
    table[...] = jnp.zeros(table.shape, jnp.float32)
    table[: active.shape[0], :] = active[...].astype(jnp.float32)
    for row, vector in zip((START, END, PENALTY, STEP), vectors):
        table[row : row + 1, :] = vector[...].astype(jnp.float32)
    by_gene[...] = table[...].T
    low, high = slice(0, OWN), slice(OWN, 2 * OWN)
    width = coef.shape[1]
    for block in range(width // LANES):
        cols = slice(block * LANES, (block + 1) * LANES)
        mask = block_mask(where, by_gene[...], block, width // 4)
        coef[:, cols] = (mask * coef_start[:, cols]).astype(jnp.bfloat16)
        for part, hop in ((low, 0), (high, MIRROR)):
            rows = rows_of(person(where), hop)
            mask = block_mask(where, by_gene[rows, :], block, width // 4)
            coef_own[part, cols] = mask * coef_start[rows, cols]


def gradient(total, near, far, half, cols, used):
    part, other = slice(half * OWN, (half + 1) * OWN), slice((1 - half) * OWN, (2 - half) * OWN)
    sums = near[part, cols].astype(jnp.float32) + far[other, cols].astype(jnp.float32)
    return sums / total - used.astype(jnp.float32)


def update_kernel(total, first, where, by_gene, near, far, coef_own, base, *refs):
    width = coef_own.shape[1]
    for half, hop in enumerate((0, MIRROR)):
        rows, part = rows_of(person(where), hop), slice(half * OWN, (half + 1) * OWN)
        table = by_gene[rows, :]
        penalty, step = table[:, PENALTY : PENALTY + 1], table[:, STEP : STEP + 1]
        cut = step * penalty
        for block in range(width // LANES):
            cols = slice(block * LANES, (block + 1) * LANES)
            mask = block_mask(where, table, block, width // 4)
            used = base[rows, cols] if first else base[part, cols]
            moved = coef_own[part, cols] + step * gradient(total, near, far, half, cols, used)
            size = jnp.maximum(jnp.abs(moved) - cut * l1_share, 0.0)
            kept = mask * jnp.where(moved < 0, -size, size) / (1.0 + cut * (1.0 - l1_share))
            if first:
                refs[0][part, cols] = kept
            refs[-1][part, cols] = kept.astype(jnp.bfloat16)
    if not first:
        refs[-1][:, width:] = refs[0][...]


def peaks_kernel(total, where, by_gene, near, far, base, out):
    width = near.shape[1]
    lane = lax.broadcasted_iota(jnp.int32, (OWN, LANES), 1)
    for half, hop in enumerate((0, MIRROR)):
        rows = rows_of(person(where), hop)
        table = by_gene[rows, :]
        high = low = jnp.zeros((OWN, LANES), jnp.float32)
        for block in range(width // LANES):
            cols = slice(block * LANES, (block + 1) * LANES)
            mask = block_mask(where, table, block, width // 4)
            grad = gradient(total, near, far, half, cols, base[rows, cols])
            scaled = mask * jnp.abs(grad) / table[:, PENALTY : PENALTY + 1]
            peak = jnp.max(scaled, axis=1, keepdims=True)
            rounded = peak.astype(jnp.bfloat16).astype(jnp.float32)
            high = jnp.where(lane == block, rounded, high)
            low = jnp.where(lane == block + width // LANES, peak - rounded, low)
        out[half * OWN : (half + 1) * OWN, :] = (high + low).astype(jnp.bfloat16)


def output_kernel(where, *refs):
    *pieces, out, peaks, tail = refs
    width = out.shape[1]

    def put(rows, piece):
        out[rows, :] = piece[:, :width].astype(jnp.float32)
        tail[rows, :] = piece[:, width:].astype(jnp.float32)

    place(person(where), pieces, put)
    count = peaks.shape[0]
    flat = tail[...].T
    peaks[...] = flat[:count, :] + flat[count : 2 * count, :]


def in_vmem(array):
    return pltpu.with_memory_space_constraint(array, pltpu.VMEM)


def specs(count):
    vmem = pl.BlockSpec(memory_space=pltpu.VMEM)
    return [pl.BlockSpec(memory_space=pltpu.SMEM)] + [vmem] * count


def cut_columns(where, genotypes, reach):
    half = pltpu.VMEM((genotypes.shape[0], reach), genotypes.dtype)
    return pl.pallas_call(
        cut_kernel,
        out_shape=[half, half],
        in_specs=[pl.BlockSpec(memory_space=pltpu.SMEM), pl.BlockSpec(memory_space=pltpu.HBM)],
        out_specs=[pl.BlockSpec(memory_space=pltpu.VMEM)] * 2,
        scratch_shapes=[pltpu.SemaphoreType.DMA((2 * COPIES,))],
        compiler_params=pltpu.CompilerParams(vmem_limit_bytes=8 << 20),
    )(where, pltpu.with_memory_space_constraint(genotypes, pltpu.HBM))


def cost(people, blocks, products):
    flops = 2 * products * people * blocks.shape[0] * blocks.shape[1]
    return pl.CostEstimate(flops=flops, bytes_accessed=0, transcendentals=0)


def early_part(where, blocks, target, coef):
    operands = [in_vmem(v) for v in (*blocks, target, coef)]
    return pl.pallas_call(
        early_kernel,
        out_shape=pltpu.VMEM(target.shape, jnp.float32),
        in_specs=specs(len(operands)),
        out_specs=pl.BlockSpec(memory_space=pltpu.VMEM),
        compiler_params=pltpu.CompilerParams(vmem_limit_bytes=8 << 20),
        cost_estimate=pl.CostEstimate(flops=0, bytes_accessed=0, transcendentals=0),
    )(where, *operands)


def local_grad(where, blocks, target, pieces):
    people, genes = target.shape
    width = 4 * blocks[0].shape[1]
    operands = [in_vmem(v) for v in (*blocks, target, *pieces)]
    outs = [pltpu.VMEM((2 * OWN * len(NEAR), width), jnp.float32)]
    outs += [pltpu.VMEM((2 * OWN * len(hops), width), jnp.bfloat16) for hops in GIVE]
    scratch = [pltpu.VMEM((genes, width), jnp.float32), pltpu.VMEM((genes, people), jnp.bfloat16)]
    if len(pieces) > 1:
        scratch.append(pltpu.VMEM((genes, width), jnp.bfloat16))
    return pl.pallas_call(
        functools.partial(turn_kernel, len(pieces)),
        out_shape=outs,
        in_specs=specs(len(operands)),
        out_specs=[pl.BlockSpec(memory_space=pltpu.VMEM)] * len(outs),
        scratch_shapes=scratch,
        compiler_params=pltpu.CompilerParams(vmem_limit_bytes=20 << 20),
        cost_estimate=cost(people, jax.ShapeDtypeStruct((genes, width), jnp.bfloat16), 2),
    )(where, *operands)


def small_call(kernel, where, operands, outs, scratch=()):
    return pl.pallas_call(
        kernel,
        out_shape=[pltpu.VMEM(shape, dtype) for shape, dtype in outs],
        in_specs=specs(len(operands)),
        out_specs=[pl.BlockSpec(memory_space=pltpu.VMEM)] * len(outs),
        scratch_shapes=list(scratch),
        compiler_params=pltpu.CompilerParams(vmem_limit_bytes=8 << 20),
    )(where, *[in_vmem(v) for v in operands])


def swap(block, hop):
    count = lax.axis_size("people")
    return lax.ppermute(block, "people", [(i, i ^ hop) for i in range(count)])


def sum_to_owner(keep, gives):
    part = {}
    for hops, give in zip(GIVE, gives):
        if hops == GIVE[-1]:
            give, *_ = lax.optimization_barrier((give, got))
        got = swap(give, SIDE)
        for n, hop in enumerate(hops):
            at = NEAR.index(hop) * 2 * OWN
            part[hop] = keep[at : at + 2 * OWN] + got[2 * n * OWN : 2 * (n + 1) * OWN]
    total = part[0]
    for hop in (6, 4, 2):
        total = total + swap(part[hop].astype(jnp.bfloat16), hop)
    near = total.astype(jnp.bfloat16)
    return near, swap(near, MIRROR)


def gather_rows(pair):
    got = {0: pair, 2: swap(pair, 2), 6: swap(pair, 6)}
    beside = swap(pair, SIDE)
    pair, *_ = lax.optimization_barrier((pair, got[6], beside))
    got[4] = swap(pair, 4)
    return [got[hop] for hop in NEAR] + [beside] + [swap(got[hop], SIDE) for hop in NEAR[1:]]


def on_device(
    genotypes, expression, coef_start, penalty, step_size, window_start, window_end, active_blocks
):
    v_local = genotypes.shape[1]
    total = genotypes.shape[0] * lax.axis_size("people")
    genes, width = coef_start.shape
    reach = (width - v_local) // 2
    count = lax.axis_size("genome")
    sibling = [(i, i ^ 1) for i in range(count)]
    beyond = [(i, i + 1 if i % 2 else i - 1) for i in range(count)]
    beyond = [(source, target) for source, target in beyond if 0 <= target < count]
    where = lax.axis_index(("genome", "people")).astype(jnp.int32)[None]
    vectors = [v[None] for v in (window_start, window_end, penalty, step_size)]
    by_gene, coef, coef_own = small_call(
        start_kernel,
        where,
        [active_blocks.T, *vectors, coef_start],
        [((genes, LANES), jnp.float32), ((genes, width), jnp.bfloat16), ((2 * OWN, width), jnp.float32)],
        [pltpu.VMEM((LANES, genes), jnp.float32)],
    )

    away, beside = cut_columns(where, genotypes, reach)
    slow = lax.ppermute(away, "genome", beyond)
    fast = lax.ppermute(beside, "genome", sibling)
    blocks = [slow, away, beside, fast]
    part = early_part(where, blocks[1:], expression, coef)
    keep, *gives = local_grad(where, blocks, part, [coef])
    near, far = sum_to_owner(keep, gives)
    coef_own, sent = small_call(
        functools.partial(update_kernel, total, True),
        where,
        [by_gene, near, far, coef_own, coef],
        [((2 * OWN, width), jnp.float32), ((2 * OWN, width), jnp.bfloat16)],
    )
    pieces = gather_rows(sent)
    (tail,) = small_call(
        functools.partial(peaks_kernel, total),
        where,
        [by_gene, near, far, coef],
        [((2 * OWN, LANES), jnp.bfloat16)],
    )

    keep, *gives = local_grad(where, blocks, expression, pieces)
    near, far = sum_to_owner(keep, gives)
    (last,) = small_call(
        functools.partial(update_kernel, total, False),
        where,
        [by_gene, near, far, coef_own, sent, tail],
        [((2 * OWN, width + LANES), jnp.bfloat16)],
    )
    pieces = gather_rows(last)
    coef, peaks = pl.pallas_call(
        output_kernel,
        out_shape=[
            jax.ShapeDtypeStruct((genes, width), jnp.float32),
            jax.ShapeDtypeStruct((width // LANES, genes), jnp.float32),
        ],
        in_specs=specs(len(pieces)),
        out_specs=[pl.BlockSpec(memory_space=pltpu.VMEM)] * 2,
        scratch_shapes=[pltpu.VMEM((genes, LANES), jnp.float32)],
        compiler_params=pltpu.CompilerParams(vmem_limit_bytes=8 << 20),
    )(where, *[in_vmem(piece) for piece in pieces])
    return (coef, peaks.T)


def solution(mesh):
    return jax.shard_map(
        on_device,
        mesh=mesh,
        in_specs=(
            P("people", "genome"),
            P("people", "genome"),
            P("genome", None),
            P("genome"),
            P("genome"),
            P("genome"),
            P("genome"),
            P("genome", None),
        ),
        out_specs=(P("genome", None), P("genome", None)),
        check_vma=False,
    )
```
